128 devices in a mesh: space: 16 (over y, x_lo, core), sample: 8 (over z, x_hi).
Axes of the slice: x: 4 (x_hi: 2, x_lo: 2; x = x_hi * 2 + x_lo), y: 4, z: 4, core: 2. Of those that a mesh axis runs over, the one named last changes fastest.
Arguments:
- fields: bfloat16 [8, 64, 20, 8192], P('sample', 'space'), may hold values from -6 to 6
- cotangent: bfloat16 [8, 64, 20, 8192], P('sample', 'space'), may hold values from -6 to 6
- spectral_weight: bfloat16 [2, 20, 20, 4608], P(None, None, None, 'space'), may hold values from -6 to 6
- point_weight: bfloat16 [20, 20], replicated, may hold values from -1.25 to 1.25
- point_bias: float32 [20], replicated, may hold values from -1 to 1
Outputs:
- activated: bfloat16 [8, 64, 20, 8192], P('sample', 'space')
- grad_input: bfloat16 [8, 64, 20, 8192], P('sample', 'space')
- grad_spectral: float32 [2, 20, 20, 4608], P(None, None, None, ('space', 'sample'))
The draws below stay inside these ranges and needn't reach their ends.
All inputs are finite; a program needn't handle non-finite values.
Results may differ from the reference program's by a relative error of at most 0.001.
Values sent between devices are 32-bit elements; how exact they have to be, the bound alone decides.
No kernel may reach another device: no remote copies, remote signals or barrier semaphores. Data moves between devices by JAX's collectives and lax.ppermute only.
A program may use at most 128 MiB of HBM per device.

```python
import math
import jax
import jax.numpy as jnp
from jax import lax

NX = 64
NY = 64
NZ = 32
NT = 4
C = 20
MX = 12
MY = 12
MZ = 8
MT = 4
SAMPLES = 8
CELLS = 8192
MODES = 4608


def level_of(stream_key, extent, cuts, smallest, top_value):
    gain, own = 1.0, jax.random.fold_in(stream_key, 6)
    for axis_at, blocks in cuts:
        steps = jnp.exp(jax.random.uniform(jax.random.fold_in(own, axis_at), (blocks,), jnp.float32, smallest / len(cuts), top_value / len(cuts)))
        gain = gain * jnp.repeat(steps, extent[axis_at] // blocks).reshape([-1 if axis == axis_at else 1 for axis in range(len(extent))])
    return gain


def scatter_about(own_key, extent, width, limit, pieces=(), kind=jnp.bfloat16):
    factor_of = level_of(own_key, extent, pieces, -0.22, 0.18) if pieces else 1.0
    result = jax.random.normal(own_key, extent, jnp.float32) * width * factor_of
    return jnp.minimum(jnp.maximum(result, -limit), limit).astype(kind)


def setup_inputs(seed: int = 0) -> dict:
    arg_keys = jax.random.split(jax.random.key(seed), 6)
    return {
        "fields": scatter_about(arg_keys[0], (SAMPLES, NX, C, CELLS), 1.0, 6.0, ((0, 8), (1, 16))),
        "cotangent": scatter_about(arg_keys[1], (SAMPLES, NX, C, CELLS), 1.0, 6.0, ((0, 8), (1, 16))),
        "spectral_weight": scatter_about(arg_keys[2], (2, C, C, MODES), 1.0, 6.0, ((3, 16),)),
        "point_weight": scatter_about(arg_keys[3], (C, C), C ** -0.5, 1.25),
        "point_bias": jnp.clip(jax.random.uniform(arg_keys[4], (C,), jnp.float32, -1.0, 1.0), -1.0, 1.0),
    }


def kept_index(length, modes):
    index = jnp.arange(modes, dtype=jnp.int32)
    return jnp.where(index < modes // 2, index, length - modes + index)

def mode_indices():
    index_x = kept_index(NX, MX)[:, None, None, None]
    index_y = kept_index(NY, MY)[None, :, None, None]
    index_z = kept_index(NZ, MZ)[None, None, :, None]
    index_t = kept_index(NT, MT)[None, None, None, :]
    return (index_x, index_y, index_z, index_t)

def to_grid(planes):
    return jnp.transpose(planes, (1, 0, 2)).reshape(planes.shape[1], NX, NY, NZ, NT)

def from_grid(lattice):
    return jnp.transpose(lattice.reshape(lattice.shape[0], NX, NY * NZ * NT), (1, 0, 2))

def select_modes(spectrum):
    index_x, index_y, index_z, index_t = mode_indices()
    picked = spectrum[:, index_x, index_y, index_z, index_t]
    return jnp.transpose(picked, (0, 3, 4, 2, 1)).reshape(spectrum.shape[0], MZ * MT * MY * MX)

def place_modes(coeffs):
    index_x, index_y, index_z, index_t = mode_indices()
    arranged = jnp.transpose(coeffs.reshape(coeffs.shape[0], MZ, MT, MY, MX), (0, 4, 3, 1, 2))
    empty = jnp.zeros((coeffs.shape[0], NX, NY, NZ, NT), dtype=coeffs.dtype)
    return empty.at[:, index_x, index_y, index_z, index_t].set(arranged)

def gelu_slope(values):
    return 0.5 * (1.0 + lax.erf(values * (1.0 / math.sqrt(2.0)))) + values * jnp.exp(-0.5 * values * values) * (1.0 / math.sqrt(2.0 * math.pi))

def reference(fields, cotangent, spectral_weight, point_weight, point_bias):
    volume = NX * NY * NZ * NT
    weights = spectral_weight.astype(jnp.float32)
    mixer_full = weights[0] + 1j * weights[1]
    mixer_conj = weights[0] - 1j * weights[1]
    point_mat = point_weight.astype(jnp.float32)
    bias_vec = point_bias.astype(jnp.float32)
    highest = lax.Precision.HIGHEST

    def per_sample(running, inputs_pair):
        sample_field, sample_cot = inputs_pair
        values = sample_field.astype(jnp.float32)
        spec_in = select_modes(jnp.fft.fftn(to_grid(values), axes=(1, 2, 3, 4)))
        mixed = jnp.einsum('com,cm->om', mixer_full, spec_in, precision=highest)
        spectral = from_grid(jnp.real(jnp.fft.ifftn(place_modes(mixed), axes=(1, 2, 3, 4))))
        local = jnp.einsum('xcn,co->xon', values, point_mat, precision=highest)
        pre = spectral + local + bias_vec[None, :, None]
        activated = jax.nn.gelu(pre, approximate=False).astype(jnp.bfloat16)
        upstream = sample_cot.astype(jnp.float32) * gelu_slope(pre)
        spec_up = select_modes(jnp.fft.fftn(to_grid(upstream), axes=(1, 2, 3, 4))) / volume
        back = jnp.einsum('com,om->cm', mixer_conj, spec_up, precision=highest)
        spectral_back = from_grid(jnp.real(jnp.fft.ifftn(place_modes(back), axes=(1, 2, 3, 4)))) * volume
        grad_in = (spectral_back + jnp.einsum('xon,co->xcn', upstream, point_mat, precision=highest)).astype(jnp.bfloat16)
        grad_term = jnp.conj(spec_in)[:, None, :] * spec_up[None, :, :]
        running = running + jnp.stack([jnp.real(grad_term), jnp.imag(grad_term)]).astype(jnp.float32)
        return (running, (activated, grad_in))
    initial = jnp.zeros((2, C, C, MZ * MT * MY * MX), jnp.float32)
    running, outputs = lax.scan(per_sample, initial, (fields, cotangent))
    return (outputs[0], outputs[1], running)
```

```python
import functools
import math

import jax
import jax.numpy as jnp
import ml_dtypes
import numpy as np
from jax import lax
from jax.experimental import pallas as pl
from jax.experimental.pallas import tpu as pltpu
from jax.sharding import PartitionSpec as P

NX, NY, NZ, NT = 64, 64, 32, 4
MX, MY, MZ, MT = 12, 12, 8, 4
C = 20
CP = 24
PLANE = NZ * NT
CELLS = NY * PLANE
KEPT_ROWS = C * MY
SLAB = 4
OWNERS = 16
SAMPLES = 8
BLOCK_MODES = 36
PAIRS = C // 2
CHUNK = 8
VOLUME = NX * NY * NZ * NT
F32, BF16 = jnp.float32, jnp.bfloat16
VMEM_LIMIT = 24 * 1024 * 1024


def signed(index, modes):
    return np.where(index < modes // 2, index, index - modes)


def hi_lo(table):
    hi = table.astype(np.float32).astype(ml_dtypes.bfloat16)
    lo = (table - hi.astype(np.float64)).astype(np.float32).astype(ml_dtypes.bfloat16)
    return hi, lo


def y_table():
    k = signed(np.arange(MY), MY)[:, None]
    theta = 2 * np.pi * ((k * np.arange(NY)[None, :]) % NY) / NY
    eye = np.eye(2)
    return np.concatenate([np.kron(eye, np.cos(theta)), np.kron(eye, -np.sin(theta))], axis=0)


def plane_table():
    z = np.arange(PLANE) // NT
    t = np.arange(PLANE) % NT
    rows = []
    for ql in range(2):
        q = 2 * np.arange(OWNERS) + ql
        fz = signed(q // MT, MZ)[:, None]
        ft = signed(q % MT, MT)[:, None]
        phase = (fz * z * NT + ft * t * NZ) % PLANE
        theta = 2 * np.pi * phase / PLANE
        rows.append(np.concatenate([np.cos(theta), np.sin(theta)], axis=1))
        rows.append(np.concatenate([-np.sin(theta), np.cos(theta)], axis=1))
    return np.concatenate(rows, axis=0)


def x_tables(ql, forward_scale, inverse_scale):
    lane = np.arange(256) + 128 * ql
    f = signed(lane % MX, MX)[None, :]
    theta = 2 * np.pi * ((f * np.arange(NX)[:, None]) % NX) / NX
    cos, sin = np.cos(theta), np.sin(theta)
    forward = np.zeros((NX, 2, 512))
    forward[:, 0] = np.concatenate([cos, -sin], axis=1)
    forward[:, 1] = np.concatenate([sin, cos], axis=1)
    inverse = np.zeros((NX, 2, 512))
    inverse[:, 0] = np.concatenate([cos, -sin], axis=1)
    inverse[:, 1] = np.concatenate([sin, cos], axis=1)
    return forward.reshape(128, 512) * forward_scale, inverse.reshape(128, 512) * inverse_scale


def mode_mask():
    mask = np.zeros((2, 24, 512), np.float32)
    for ql in range(2):
        lane = np.arange(256) + 128 * ql
        code = np.where(lane < 288, lane // MX, -1)
        hit = code[None, :] == (ql * MY + np.arange(24)[:, None] % MY)
        mask[ql] = np.concatenate([hit, hit], axis=1)
    return mask


def group_table():
    g = np.zeros((CP, KEPT_ROWS), np.float32)
    for c in range(C):
        g[c, c * MY : (c + 1) * MY] = 1.0
    return g


def split(value):
    hi = value.astype(BF16)
    return hi, (value - hi.astype(F32)).astype(BF16)


def dot(a, b):
    return lax.dot_general(a, b, (((1,), (0,)), ((), ())), preferred_element_type=F32)


def dot_tn(a, b):
    return lax.dot_general(a, b, (((0,), (0,)), ((), ())), preferred_element_type=F32)


def dot_nt(a, b):
    return lax.dot_general(a, b, (((1,), (1,)), ((), ())), preferred_element_type=F32)


def slab_forward(tile_ref, exact, x, ytab, ztab, out_ref):
    real, imag = [], []
    for p in range(PAIRS):
        cells = tile_ref[p * 128 : (p + 1) * 128, :]
        if exact:
            both = dot(ytab[...], cells.astype(BF16))
            u = both[:48] + both[48:]
        else:
            hi, lo = split(cells)
            both = dot(ytab[...], hi)
            u = both[:48] + both[48:] + dot(ytab[:48], lo)
        real.append(u[:24])
        imag.append(u[24:])
    fill = [jnp.zeros((256 - KEPT_ROWS, 128), F32)]
    rows = jnp.concatenate(
        [jnp.concatenate(real + fill, axis=0), jnp.concatenate(imag + fill, axis=0)], axis=1
    )
    hi, lo = split(rows)
    both = dot_nt(ztab[...], hi)
    out = both[:64] + both[64:] + dot_nt(ztab[:64], lo)
    for ql in range(2):
        for reim in range(2):
            at = (ql * 2 + reim) * 16
            for half in range(2):
                start = (ql * 2 + half) * 8 + x * 2 + reim
                out_ref[pl.ds(start, OWNERS, stride=32), :] = out[at : at + 16, half * 128 : (half + 1) * 128]


def slab_inverse(recv_ref, x, ytab_t, ztab_k, tile_ref):
    parts = []
    for ql in range(2):
        for reim in range(2):
            halves = [
                recv_ref[pl.ds((ql * 2 + half) * 8 + x * 2 + reim, OWNERS, stride=32), :] for half in range(2)
            ]
            parts.append(jnp.concatenate(halves, axis=1))
    hi, lo = split(jnp.concatenate(parts, axis=0))
    h = dot_tn(jnp.concatenate([hi, lo, hi], axis=0), ztab_k[...])
    for p in range(PAIRS):
        pair = h[p * 24 : (p + 1) * 24]
        hi, lo = split(jnp.concatenate([pair[:, :128], pair[:, 128:]], axis=0))
        tile_ref[p * 128 : (p + 1) * 128, :] = dot(ytab_t[...], jnp.concatenate([hi, lo, hi], axis=0))


def forward_kernel(x_ref, ytab, ztab, out_ref, tile_ref):
    x = pl.program_id(0)
    for y in range(NY):
        tile_ref[pl.ds(y, C, stride=NY), :] = x_ref[:, y * 128 : (y + 1) * 128].astype(F32)
    slab_forward(tile_ref, True, x, ytab, ztab, out_ref)


def middle_kernel(
    recv_ref, x_ref, cot_ref, wt_ref, bias_ref, ytab, ztab, ytab_t, ztab_k,
    act_ref, up_ref, out_ref, tile_ref,
):
    x = pl.program_id(0)
    slab_inverse(recv_ref, x, ytab_t, ztab_k, tile_ref)
    wt = wt_ref[...]
    bias = bias_ref[...]

    def step(i, carry):
        base = pl.multiple_of(i * (CHUNK * 128), CHUNK * 128)
        local = dot(wt, x_ref[:, pl.ds(base, CHUNK * 128)])
        for k in range(CHUNK):
            y = i * CHUNK + k
            lanes = pl.ds(pl.multiple_of(base + k * 128, 128), 128)
            pre = tile_ref[pl.ds(y, C, stride=NY), :] + local[:, k * 128 : (k + 1) * 128] + bias
            cdf = 0.5 * (1.0 + lax.erf(pre * (1.0 / math.sqrt(2.0))))
            slope = cdf + pre * jnp.exp(-0.5 * pre * pre) * (1.0 / math.sqrt(2.0 * math.pi))
            act_ref[:, lanes] = (pre * cdf).astype(BF16)
            up = cot_ref[:, lanes].astype(F32) * slope
            up_ref[:, lanes] = up
            tile_ref[pl.ds(y, C, stride=NY), :] = up
        return carry

    lax.fori_loop(0, NY // CHUNK, step, 0)
    slab_forward(tile_ref, False, x, ytab, ztab, out_ref)


def last_kernel(recv_ref, up_ref, w_ref, ytab_t, ztab_k, out_ref, tile_ref):
    x = pl.program_id(0)
    slab_inverse(recv_ref, x, ytab_t, ztab_k, tile_ref)
    w = w_ref[...]

    def step(i, carry):
        base = pl.multiple_of(i * (CHUNK * 128), CHUNK * 128)
        hi, lo = split(up_ref[:, pl.ds(base, CHUNK * 128)])
        local = dot(w, hi) + dot(w, lo)
        for k in range(CHUNK):
            lanes = pl.ds(pl.multiple_of(base + k * 128, 128), 128)
            spectral = tile_ref[pl.ds(i * CHUNK + k, C, stride=NY), :]
            out_ref[:, lanes] = (spectral + local[:, k * 128 : (k + 1) * 128]).astype(BF16)
        return carry

    lax.fori_loop(0, NY // CHUNK, step, 0)


def owner_kernel(adjoint, s_ref, w_ref, dhi, dlo, ihi, ilo, mask_ref, g_ref, gt_ref, out_ref, spec_ref, f_ref, m_ref):
    g = g_ref[...]
    halves = []
    for ql in range(2):
        tiles = [s_ref[:, t * 8 : (t + 1) * 8, :].reshape(128, 128) for t in (2 * ql, 2 * ql + 1)]
        hi, lo = split(jnp.concatenate(tiles, axis=1))
        rep = dot_tn(hi, dhi[ql]) + dot_tn(lo, dhi[ql]) + dot_tn(hi, dlo[ql])
        rep = rep[:KEPT_ROWS].reshape(PAIRS, 24, 512) * mask_ref[ql][None]
        hi, lo = split(rep.reshape(KEPT_ROWS, 512))
        halves.append(dot(g, hi) + dot(g, lo))
    for reim in range(2):
        a = halves[0][:, reim * 256 : (reim + 1) * 256]
        b = halves[1][:, reim * 256 : (reim + 1) * 256]
        f_ref[reim] = jnp.concatenate([a[:, :128], a[:, 128:] + b[:, :128], b[:, 128:]], axis=1)
    for j in range(SAMPLES):
        for reim in range(2):
            spec_ref[j, :, reim * 64 : reim * 64 + BLOCK_MODES] = f_ref[
                reim, :, j * BLOCK_MODES : (j + 1) * BLOCK_MODES
            ]
    m_ref[...] = jnp.zeros_like(m_ref)
    if adjoint:
        fr, fi = f_ref[0, :C, :288], f_ref[1, :C, :288]
        for c in range(C):
            wr, wi = w_ref[c].astype(F32), w_ref[C + c].astype(F32)
            m_ref[0, c : c + 1, :288] = jnp.sum(wr * fr + wi * fi, axis=0, keepdims=True)
            m_ref[1, c : c + 1, :288] = jnp.sum(wr * fi - wi * fr, axis=0, keepdims=True)
    else:
        mr = jnp.zeros((C, 288), F32)
        mi = jnp.zeros((C, 288), F32)
        for c in range(C):
            wr, wi = w_ref[c].astype(F32), w_ref[C + c].astype(F32)
            fr, fi = f_ref[0, c : c + 1, :288], f_ref[1, c : c + 1, :288]
            mr = mr + (wr * fr - wi * fi)
            mi = mi + (wr * fi + wi * fr)
        m_ref[0, :C, :288] = mr
        m_ref[1, :C, :288] = mi
    for ql in range(2):
        lanes = slice(ql * 128, ql * 128 + 256)
        hi, lo = split(jnp.concatenate([m_ref[0, :, lanes], m_ref[1, :, lanes]], axis=1))
        mask = mask_ref[ql][None]
        spread = []
        for part in (hi, lo):
            rows = dot(gt_ref[...], part).reshape(PAIRS, 24, 512) * mask
            rows = jnp.concatenate([rows.reshape(KEPT_ROWS, 512), jnp.zeros((256 - KEPT_ROWS, 512), F32)], axis=0)
            spread.append(rows.astype(BF16))
        hi, lo = spread
        out = dot_nt(ihi[ql], hi) + dot_nt(ihi[ql], lo) + dot_nt(ilo[ql], hi)
        for half in range(2):
            t = 2 * ql + half
            out_ref[:, t * 8 : (t + 1) * 8, :] = out[:, half * 128 : (half + 1) * 128].reshape(OWNERS, 8, 128)


def weight_kernel(a_ref, b_ref, out_ref):
    low = lax.broadcasted_iota(jnp.int32, (CP, 128), 1) < 64
    terms = []
    for s in range(SAMPLES):
        a, b = a_ref[s], b_ref[s]
        turned, b_turned = pltpu.roll(a, 64, 1), pltpu.roll(b, 64, 1)
        terms.append(
            (jnp.where(low, a, turned), jnp.where(low, turned, a), b, jnp.where(low, b_turned, -b_turned))
        )
    for c in range(C):
        total = jnp.zeros((CP, 128), F32)
        for re, im, b, swapped in terms:
            total = total + (re[c : c + 1] * b + im[c : c + 1] * swapped)
        out_ref[0, c] = total[:C, :BLOCK_MODES]
        out_ref[1, c] = total[:C, 64 : 64 + BLOCK_MODES]


def whole(shape):
    return pl.BlockSpec(shape, lambda *_: (0,) * len(shape))


def plane_spec(ndim_lead):
    return pl.BlockSpec((None,) * ndim_lead + (C, CELLS), lambda x: (0,) * (ndim_lead - 1) + (x, 0, 0))


def params():
    return pltpu.CompilerParams(vmem_limit_bytes=VMEM_LIMIT)


def exchange(block):
    return lax.all_to_all(block, "space", split_axis=0, concat_axis=0, tiled=True)


def shards(fields, cotangent, spectral_weight, point_weight, point_bias):
    yhi, ylo = hi_lo(y_table())
    zhi, zlo = hi_lo(plane_table())
    ytab = jnp.asarray(np.concatenate([yhi, ylo], axis=0))
    ztab = jnp.asarray(np.concatenate([zhi, zlo], axis=0))
    ytab_t = jnp.asarray(np.concatenate([yhi.T, yhi.T, ylo.T], axis=1))
    ztab_k = jnp.asarray(np.concatenate([zhi, zhi, zlo], axis=0))
    mask = jnp.asarray(mode_mask())
    g = jnp.asarray(group_table().astype(ml_dtypes.bfloat16))
    gt = jnp.asarray(group_table().T.astype(ml_dtypes.bfloat16))
    flat = (OWNERS * 32, 128)
    slab_out = jax.ShapeDtypeStruct(flat, F32)
    owned_out = jax.ShapeDtypeStruct((OWNERS, 32, 128), F32)
    table_specs = [whole(ytab.shape), whole(ztab.shape)]
    inverse_specs = [whole(ytab_t.shape), whole(ztab_k.shape)]
    tile = pltpu.VMEM((C * NY, 128), F32)

    def owner(received, adjoint):
        scale = 1.0 / VOLUME
        tabs = [x_tables(ql, scale if adjoint else 1.0, 1.0 if adjoint else scale) for ql in range(2)]
        dhi, dlo = hi_lo(np.stack([t[0] for t in tabs]))
        ihi, ilo = hi_lo(np.stack([t[1] for t in tabs]))
        weights = spectral_weight.reshape(2 * C, C, 288)
        return pl.pallas_call(
            functools.partial(owner_kernel, adjoint),
            out_shape=[owned_out, jax.ShapeDtypeStruct((SAMPLES, CP, 128), F32)],
            scratch_shapes=[pltpu.VMEM((2, CP, 384), F32), pltpu.VMEM((2, CP, 384), F32)],
            compiler_params=params(),
            name="owner_up" if adjoint else "owner_in",
        )(received, weights, jnp.asarray(dhi), jnp.asarray(dlo), jnp.asarray(ihi), jnp.asarray(ilo), mask, g, gt)

    sent = pl.pallas_call(
        forward_kernel,
        grid=(SLAB,),
        in_specs=[plane_spec(2)] + table_specs,
        out_specs=whole(flat),
        out_shape=slab_out,
        scratch_shapes=[tile],
        compiler_params=params(),
        name="slab_in",
    )(fields, ytab, ztab)
    mixed, spec_in = owner(exchange(sent.reshape(OWNERS, 32, 128)), False)
    bias = jnp.broadcast_to(point_bias[:, None], (C, 128))
    activated, upstream, sent = pl.pallas_call(
        middle_kernel,
        grid=(SLAB,),
        in_specs=[whole(flat), plane_spec(2), plane_spec(2), whole((C, C)), whole((C, 128))]
        + table_specs
        + inverse_specs,
        out_specs=[plane_spec(2), plane_spec(1), whole(flat)],
        out_shape=[
            jax.ShapeDtypeStruct((1, SLAB, C, CELLS), BF16),
            jax.ShapeDtypeStruct((SLAB, C, CELLS), F32),
            slab_out,
        ],
        scratch_shapes=[tile],
        compiler_params=params(),
        name="slab_mid",
    )(exchange(mixed).reshape(flat), fields, cotangent, point_weight.T, bias, ytab, ztab, ytab_t, ztab_k)
    back, spec_up = owner(exchange(sent.reshape(OWNERS, 32, 128)), True)
    grad_input = pl.pallas_call(
        last_kernel,
        grid=(SLAB,),
        in_specs=[whole(flat), plane_spec(1), whole((C, C))] + inverse_specs,
        out_specs=plane_spec(2),
        out_shape=jax.ShapeDtypeStruct((1, SLAB, C, CELLS), BF16),
        scratch_shapes=[tile],
        compiler_params=params(),
        name="slab_out",
    )(exchange(back).reshape(flat), upstream, point_weight, ytab_t, ztab_k)
    both = jnp.concatenate([spec_in, spec_up], axis=1)
    both = lax.all_to_all(both, "sample", split_axis=0, concat_axis=0, tiled=True)
    grad_spectral = pl.pallas_call(
        weight_kernel,
        out_shape=jax.ShapeDtypeStruct((2, C, C, BLOCK_MODES), F32),
        compiler_params=params(),
        name="weight_grad",
    )(both[:, :CP], both[:, CP:])
    return activated, grad_input, grad_spectral


def solution(mesh):
    return jax.shard_map(
        shards,
        mesh=mesh,
        in_specs=(
            P("sample", "space", None, None),
            P("sample", "space", None, None),
            P(None, None, None, "space"),
            P(),
            P(),
        ),
        out_specs=(
            P("sample", "space", None, None),
            P("sample", "space", None, None),
            P(None, None, None, ("space", "sample")),
        ),
        check_vma=False,
    )
```

```python
import functools
import math

import jax
import jax.numpy as jnp
import ml_dtypes
import numpy as np
from jax import lax
from jax.experimental import pallas as pl
from jax.experimental.pallas import tpu as pltpu
from jax.sharding import PartitionSpec as P

NX, NY, NZ, NT = 64, 64, 32, 4
MX, MY, MZ, MT = 12, 12, 8, 4
C = 20
CP = 24
PLANE = NZ * NT
CELLS = NY * PLANE
KEPT_ROWS = C * MY
SLAB = 4
OWNERS = 16
SAMPLES = 8
BLOCK_MODES = 36
PAIRS = C // 2
CHUNK = 64
STEPS = C // 4
ROWS = C * SLAB * NY
PAIR_ROWS = 2 * SLAB * NY
QUAD_ROWS = 2 * PAIR_ROWS
QUARTER = 2 * SLAB * 24
MIX = 16
VOLUME = NX * NY * NZ * NT
F32, BF16 = jnp.float32, jnp.bfloat16
MIB = 1024 * 1024


def signed(index, modes):
    return np.where(index < modes // 2, index, index - modes)


def hi_lo(table):
    hi = table.astype(np.float32).astype(ml_dtypes.bfloat16)
    lo = (table - hi.astype(np.float64)).astype(np.float32).astype(ml_dtypes.bfloat16)
    return hi, lo


def y_table():
    k = signed(np.arange(MY), MY)[:, None]
    theta = 2 * np.pi * ((k * np.arange(NY)[None, :]) % NY) / NY
    eye2, eye4 = np.eye(2), np.eye(SLAB)
    parts = [np.einsum("ab,pq,ky->apkqyb", eye4, eye2, t) for t in (np.cos(theta), -np.sin(theta))]
    return np.stack(parts).reshape(QUARTER, PAIR_ROWS)


def plane_table():
    z = np.arange(PLANE) // NT
    t = np.arange(PLANE) % NT
    rows = []
    for ql in range(2):
        q = 2 * np.arange(OWNERS) + ql
        fz = signed(q // MT, MZ)[:, None]
        ft = signed(q % MT, MT)[:, None]
        phase = (fz * z * NT + ft * t * NZ) % PLANE
        theta = 2 * np.pi * phase / PLANE
        rows.append(np.concatenate([np.cos(theta), np.sin(theta)], axis=1))
        rows.append(np.concatenate([-np.sin(theta), np.cos(theta)], axis=1))
    return np.concatenate(rows, axis=0)


def x_tables(ql, forward_scale, inverse_scale):
    lane = np.arange(256) + 128 * ql
    f = signed(lane % MX, MX)[None, :]
    theta = 2 * np.pi * ((f * np.arange(NX)[:, None]) % NX) / NX
    cos, sin = np.cos(theta), np.sin(theta)
    forward = np.zeros((NX, 2, 512))
    forward[:, 0] = np.concatenate([cos, -sin], axis=1)
    forward[:, 1] = np.concatenate([sin, cos], axis=1)
    inverse = np.zeros((NX, 2, 512))
    inverse[:, 0] = np.concatenate([cos, -sin], axis=1)
    inverse[:, 1] = np.concatenate([sin, cos], axis=1)
    return forward.reshape(128, 512) * forward_scale, inverse.reshape(128, 512) * inverse_scale


def mode_mask():
    mask = np.zeros((2, 24, 512), np.float32)
    for ql in range(2):
        lane = np.arange(256) + 128 * ql
        code = np.where(lane < 288, lane // MX, -1)
        hit = code[None, :] == (ql * MY + np.arange(24)[:, None] % MY)
        mask[ql] = np.concatenate([hit, hit], axis=1)
    return mask


def group_table():
    g = np.zeros((CP, KEPT_ROWS), np.float32)
    for c in range(C):
        g[c, c * MY : (c + 1) * MY] = 1.0
    return g


def split(value):
    hi = value.astype(BF16)
    return hi, (value - hi.astype(F32)).astype(BF16)


def dot(a, b):
    return lax.dot_general(a, b, (((1,), (0,)), ((), ())), preferred_element_type=F32)


def dot_tn(a, b):
    return lax.dot_general(a, b, (((0,), (0,)), ((), ())), preferred_element_type=F32)


def dot_nt(a, b):
    return lax.dot_general(a, b, (((1,), (1,)), ((), ())), preferred_element_type=F32)


def forward_y(quad, left, right, ytab, u_ref):
    u = dot(ytab[...], jnp.concatenate([left[0], right[0]], axis=1))
    u = u[:QUARTER] + u[QUARTER:]
    if len(left) > 1:
        u = u + dot(ytab[:QUARTER], jnp.concatenate([left[1], right[1]], axis=1))
    for side in range(2):
        rows = slice(quad * 48 + side * 24, quad * 48 + side * 24 + 24)
        for reim in range(2):
            for x in range(SLAB):
                at = (reim * SLAB + x) * 24
                u_ref[x, rows, reim * 128 : (reim + 1) * 128] = u[at : at + 24, side * 128 : (side + 1) * 128]


def forward_plane(u_ref, ztab, out_ref):
    for x in range(SLAB):
        u_ref[x, KEPT_ROWS:, :] = jnp.zeros((256 - KEPT_ROWS, 256), F32)
        hi, lo = split(u_ref[x])
        both = dot_nt(ztab[...], hi)
        out = both[:64] + both[64:] + dot_nt(ztab[:64], lo)
        for ql in range(2):
            for reim in range(2):
                at = (ql * 2 + reim) * 16
                for half in range(2):
                    start = (ql * 2 + half) * 8 + x * 2 + reim
                    out_ref[pl.ds(start, OWNERS, stride=32), :] = out[at : at + 16, half * 128 : (half + 1) * 128]


def inverse_plane(recv_ref, ztab_k, h_ref):
    for x in range(SLAB):
        parts = []
        for ql in range(2):
            for reim in range(2):
                halves = [
                    recv_ref[pl.ds((ql * 2 + half) * 8 + x * 2 + reim, OWNERS, stride=32), :] for half in range(2)
                ]
                parts.append(jnp.concatenate(halves, axis=1))
        hi, lo = split(jnp.concatenate(parts, axis=0))
        h_ref[x] = dot_tn(jnp.concatenate([hi, lo, hi], axis=0), ztab_k[...])


def inverse_y(quad, h_ref, ytab_t):
    pieces = []
    for reim in range(2):
        for x in range(SLAB):
            sides = [
                h_ref[x, quad * 48 + side * 24 : quad * 48 + side * 24 + 24, reim * 128 : (reim + 1) * 128]
                for side in range(2)
            ]
            pieces.append(jnp.concatenate(sides, axis=1))
    hi, lo = split(jnp.concatenate(pieces, axis=0))
    return dot(ytab_t[...], jnp.concatenate([hi, lo, hi], axis=0))


def quad_rows(quad):
    return pl.ds(quad * QUAD_ROWS, QUAD_ROWS)


def fetch(source, target, sems, first):
    copies = [
        pltpu.make_async_copy(source.at[quad_rows(q)], target.at[quad_rows(q)], sems.at[first + q])
        for q in range(STEPS)
    ]
    for copy in copies:
        copy.start()
    return copies


def forward_kernel(x_hbm, ytab_hbm, ztab_hbm, out_ref, x_ref, ytab, ztab, u_ref, sems):
    tables = [
        pltpu.make_async_copy(ytab_hbm, ytab, sems.at[STEPS]),
        pltpu.make_async_copy(ztab_hbm, ztab, sems.at[STEPS + 1]),
    ]
    tables[0].start()
    copies = fetch(x_hbm, x_ref, sems, 0)
    tables[1].start()
    tables[0].wait()
    for quad in range(STEPS):
        copies[quad].wait()
        at = quad * QUAD_ROWS
        left, right = x_ref[at : at + PAIR_ROWS, :], x_ref[at + PAIR_ROWS : at + QUAD_ROWS, :]
        forward_y(quad, [left], [right], ytab, u_ref)
    tables[1].wait()
    forward_plane(u_ref, ztab, out_ref)


def middle_kernel(
    recv_ref, local_hbm, cot_hbm, ytab, ztab, ytab_t, ztab_k,
    act_hbm, up_hbm, out_ref,
    local_ref, cot_ref, act_ref, up_ref, h_ref, u_ref, pre_ref, hi_ref, lo_ref, sems,
):
    local_copies = fetch(local_hbm, local_ref, sems, 0)
    cot_copies = fetch(cot_hbm, cot_ref, sems, STEPS)
    stores = []
    inverse_plane(recv_ref, ztab_k, h_ref)
    for quad in range(STEPS):
        pre_ref[...] = inverse_y(quad, h_ref, ytab_t)
        local_copies[quad].wait()
        cot_copies[quad].wait()
        for side in range(2):
            lanes = slice(side * 128, (side + 1) * 128)
            for i in range(PAIR_ROWS // CHUNK):
                near = slice(i * CHUNK, (i + 1) * CHUNK)
                at = quad * QUAD_ROWS + side * PAIR_ROWS + i * CHUNK
                rows = slice(at, at + CHUNK)
                pre = pre_ref[near, lanes] + local_ref[rows, :]
                cdf = 0.5 * (1.0 + lax.erf(pre * (1.0 / math.sqrt(2.0))))
                slope = cdf + pre * jnp.exp(-0.5 * pre * pre) * (1.0 / math.sqrt(2.0 * math.pi))
                act_ref[rows, :] = (pre * cdf).astype(BF16)
                up = cot_ref[rows, :].astype(F32) * slope
                up_ref[rows, :] = up
                hi_ref[near, lanes], lo_ref[near, lanes] = split(up)
        for k, (source, target) in enumerate(((act_ref, act_hbm), (up_ref, up_hbm))):
            store = pltpu.make_async_copy(
                source.at[quad_rows(quad)], target.at[quad_rows(quad)], sems.at[(2 + k) * STEPS + quad]
            )
            store.start()
            stores.append(store)
        sides = [[ref[:, side * 128 : (side + 1) * 128] for ref in (hi_ref, lo_ref)] for side in range(2)]
        forward_y(quad, sides[0], sides[1], ytab, u_ref)
    forward_plane(u_ref, ztab, out_ref)
    for store in stores:
        store.wait()


def last_kernel(recv_ref, local_hbm, ytab_t, ztab_k, out_hbm, token_ref, local_ref, out_ref, h_ref, sems):
    token_ref[...] = jnp.zeros_like(token_ref)
    local_copies = fetch(local_hbm, local_ref, sems, 0)
    stores = []
    inverse_plane(recv_ref, ztab_k, h_ref)
    for quad in range(STEPS):
        spectral = inverse_y(quad, h_ref, ytab_t)
        local_copies[quad].wait()
        for side in range(2):
            at = quad * QUAD_ROWS + side * PAIR_ROWS
            rows = slice(at, at + PAIR_ROWS)
            out_ref[rows, :] = (spectral[:, side * 128 : (side + 1) * 128] + local_ref[rows, :]).astype(BF16)
        store = pltpu.make_async_copy(
            out_ref.at[quad_rows(quad)], out_hbm.at[quad_rows(quad)], sems.at[STEPS + quad]
        )
        store.start()
        stores.append(store)
    for store in stores:
        store.wait()


def point_kernel(transposed, x_ref, w_ref, *rest):
    bias_ref, out_ref, token_ref = rest if len(rest) == 3 else (None, *rest)
    token_ref[...] = jnp.zeros_like(token_ref)
    size = C * MIX
    row = lax.broadcasted_iota(jnp.int32, (size, C), 0)
    spread = (row // MIX == lax.broadcasted_iota(jnp.int32, (size, C), 1)).astype(F32)
    offset = jnp.sum(spread * bias_ref[...], axis=1, keepdims=True) if bias_ref is not None else 0.0
    spread = spread.astype(BF16)
    wide = (dot_nt if transposed else dot)(spread, w_ref[...]).astype(BF16)
    wide = dot_nt(wide, spread)
    row = lax.broadcasted_iota(jnp.int32, (size, size), 0)
    column = lax.broadcasted_iota(jnp.int32, (size, size), 1)
    wide = jnp.where(row % MIX == column % MIX, wide, 0.0).astype(BF16)
    for block in range(SLAB * NY // (2 * MIX)):
        sides = []
        for side in range(2):
            at = (2 * block + side) * MIX
            sides.append(
                jnp.concatenate([x_ref[c * SLAB * NY + at : c * SLAB * NY + at + MIX, :] for c in range(C)], axis=0)
            )
        both = jnp.concatenate(sides, axis=1)
        if both.dtype == BF16:
            out = dot(wide, both)
        else:
            hi, lo = split(both)
            out = dot(wide, hi) + dot(wide, lo)
        out = out + offset
        for side in range(2):
            at = (2 * block + side) * MIX
            for c in range(C):
                out_ref[c * SLAB * NY + at : c * SLAB * NY + at + MIX, :] = out[
                    c * MIX : (c + 1) * MIX, side * 128 : (side + 1) * 128
                ]


def owner_kernel(adjoint, s_ref, w_ref, dhi, dlo, ihi, ilo, mask_ref, g_ref, gt_ref, *rest):
    if adjoint:
        first_ref, _, out_ref, *send_refs = rest[:8]
        f_ref, m_ref, turn_ref, b_ref = rest[8:]
        send_refs = send_refs[:4] + [send_refs[4].at[k] for k in range(4)]
    else:
        out_ref, spec_hbm, f_ref, m_ref, turn_ref, spec_ref, sem = rest
        store = pltpu.make_async_copy(spec_ref, spec_hbm, sem)
    g = g_ref[...]
    halves = []
    for ql in range(2):
        tiles = [s_ref[:, t * 8 : (t + 1) * 8, :].reshape(128, 128) for t in (2 * ql, 2 * ql + 1)]
        hi, lo = split(jnp.concatenate(tiles, axis=1))
        rep = dot_tn(hi, dhi[ql]) + dot_tn(lo, dhi[ql]) + dot_tn(hi, dlo[ql])
        rep = rep[:KEPT_ROWS].reshape(PAIRS, 24, 512) * mask_ref[ql][None]
        hi, lo = split(rep.reshape(KEPT_ROWS, 512))
        halves.append(dot(g, hi) + dot(g, lo))
    for reim in range(2):
        a = halves[0][:, reim * 256 : (reim + 1) * 256]
        b = halves[1][:, reim * 256 : (reim + 1) * 256]
        f_ref[reim] = jnp.concatenate([a[:, :128], a[:, 128:] + b[:, :128], b[:, 128:]], axis=1)
    for reim in range(2):
        for t in range(3):
            turn_ref[t, pl.ds(reim, CP, stride=2), :] = f_ref[reim, :, t * 128 : (t + 1) * 128]
    turned = jnp.concatenate([turn_ref[t, : 2 * C, :] for t in range(3)], axis=1)
    for j in range(SAMPLES):
        block = turned[:, j * BLOCK_MODES : (j + 1) * BLOCK_MODES]
        if adjoint:
            b_ref[j, :, 64 : 64 + BLOCK_MODES] = block
            b_ref[j, :, :BLOCK_MODES] = first_ref[j, :, :BLOCK_MODES]
        else:
            spec_ref[j, :, :BLOCK_MODES] = block
    if adjoint:
        me = lax.axis_index("sample")
        for d in range(SAMPLES):
            send_refs[d][...] = b_ref[jnp.bitwise_xor(me, d)]
    else:
        store.start()
    m_ref[...] = jnp.zeros_like(m_ref)
    if adjoint:
        fr, fi = f_ref[0, :C, :288], f_ref[1, :C, :288]
        for c in range(C):
            wr, wi = w_ref[c].astype(F32), w_ref[C + c].astype(F32)
            m_ref[0, c : c + 1, :288] = jnp.sum(wr * fr + wi * fi, axis=0, keepdims=True)
            m_ref[1, c : c + 1, :288] = jnp.sum(wr * fi - wi * fr, axis=0, keepdims=True)
    else:
        mr = jnp.zeros((C, 288), F32)
        mi = jnp.zeros((C, 288), F32)
        for c in range(C):
            wr, wi = w_ref[c].astype(F32), w_ref[C + c].astype(F32)
            fr, fi = f_ref[0, c : c + 1, :288], f_ref[1, c : c + 1, :288]
            mr = mr + (wr * fr - wi * fi)
            mi = mi + (wr * fi + wi * fr)
        m_ref[0, :C, :288] = mr
        m_ref[1, :C, :288] = mi
    for ql in range(2):
        lanes = slice(ql * 128, ql * 128 + 256)
        hi, lo = split(jnp.concatenate([m_ref[0, :, lanes], m_ref[1, :, lanes]], axis=1))
        mask = mask_ref[ql][None]
        spread = []
        for part in (hi, lo):
            rows = dot(gt_ref[...], part).reshape(PAIRS, 24, 512) * mask
            rows = jnp.concatenate([rows.reshape(KEPT_ROWS, 512), jnp.zeros((256 - KEPT_ROWS, 512), F32)], axis=0)
            spread.append(rows.astype(BF16))
        hi, lo = spread
        out = dot_nt(ihi[ql], hi) + dot_nt(ihi[ql], lo) + dot_nt(ilo[ql], hi)
        for half in range(2):
            t = 2 * ql + half
            out_ref[:, t * 8 : (t + 1) * 8, :] = out[:, half * 128 : (half + 1) * 128].reshape(OWNERS, 8, 128)
    if not adjoint:
        store.wait()


def weight_kernel(*refs):
    own_ref, far_ref, near_refs, (out_ref, a_ref) = refs[0], refs[1], refs[2:5], refs[6:]
    even = lax.broadcasted_iota(jnp.int32, (2 * C, 128), 0) % 2 == 0
    terms = []
    for s, ref in enumerate([own_ref, far_ref.at[0]] + [ref.at[k] for ref in near_refs for k in range(2)]):
        block = ref[...]
        a_ref[s] = block
        b = pltpu.roll(block, 64, 1)
        below, above = pltpu.roll(b, 2 * C - 1, 0), pltpu.roll(b, 1, 0)
        terms.append((b, jnp.where(even, below, -above)))
    for c in range(C):
        total = jnp.zeros((2 * C, 128), F32)
        for s, (b, swapped) in enumerate(terms):
            total = total + (a_ref[s, 2 * c : 2 * c + 1, :] * b + a_ref[s, 2 * c + 1 : 2 * c + 2, :] * swapped)
        out_ref[c * 2 * C : (c + 1) * 2 * C, :] = total[:, :BLOCK_MODES]


def whole(shape):
    return pl.BlockSpec(shape, lambda *_: (0,) * len(shape))


def pinned():
    return pl.BlockSpec(memory_space=pltpu.HBM)


def params(limit):
    return pltpu.CompilerParams(vmem_limit_bytes=int(limit * MIB))


def cost(us):
    return pl.CostEstimate(flops=int(us * 4e8), bytes_accessed=int(us * 3e6), transcendentals=0)


def exchange(block):
    return lax.all_to_all(block, "space", split_axis=0, concat_axis=0, tiled=True)


def shards(fields, cotangent, spectral_weight, point_weight, point_bias):
    yhi, ylo = hi_lo(y_table())
    zhi, zlo = hi_lo(plane_table())
    ytab = jnp.asarray(np.concatenate([yhi, ylo], axis=0))
    ztab = jnp.asarray(np.concatenate([zhi, zlo], axis=0))
    ytab_t = jnp.asarray(np.concatenate([yhi.T, yhi.T, ylo.T], axis=1))
    ztab_k = jnp.asarray(np.concatenate([zhi, zhi, zlo], axis=0))
    mask = jnp.asarray(mode_mask())
    g = jnp.asarray(group_table().astype(ml_dtypes.bfloat16))
    gt = jnp.asarray(group_table().T.astype(ml_dtypes.bfloat16))
    flat = (OWNERS * 32, 128)
    slab_out = jax.ShapeDtypeStruct(flat, F32)
    owned_out = jax.ShapeDtypeStruct((OWNERS, 32, 128), F32)
    rows_out = [jax.ShapeDtypeStruct((ROWS, 128), dtype) for dtype in (BF16, F32)]
    table_specs = [whole(ytab.shape), whole(ztab.shape)]
    inverse_specs = [whole(ytab_t.shape), whole(ztab_k.shape)]
    planes = pltpu.VMEM((SLAB, 256, 256), F32)

    def owner(received, adjoint, *first):
        scale = 1.0 / VOLUME
        tabs = [x_tables(ql, scale if adjoint else 1.0, 1.0 if adjoint else scale) for ql in range(2)]
        dhi, dlo = hi_lo(np.stack([t[0] for t in tabs]))
        ihi, ilo = hi_lo(np.stack([t[1] for t in tabs]))
        weights = spectral_weight.reshape(2 * C, C, 288)
        if adjoint:
            spec_shapes = [(2 * C, 128)] * 4 + [(4, 2 * C, 128)]
        else:
            spec_shapes = [(SAMPLES, 2 * C, 128)]
        scratch = [pltpu.VMEM((2, CP, 384), F32), pltpu.VMEM((2, CP, 384), F32), pltpu.VMEM((3, 2 * CP, 128), F32)]
        scratch.append(pltpu.VMEM((SAMPLES, 2 * C, 128), F32))
        if not adjoint:
            scratch.append(pltpu.SemaphoreType.DMA)
        return pl.pallas_call(
            functools.partial(owner_kernel, adjoint),
            out_shape=[owned_out] + [jax.ShapeDtypeStruct(shape, F32) for shape in spec_shapes],
            scratch_shapes=scratch,
            **({} if adjoint else {"out_specs": [whole(owned_out.shape), pinned()]}),
            compiler_params=params(52),
            cost_estimate=cost(3),
            name="owner_up" if adjoint else "owner_in",
        )(received, weights, *map(jnp.asarray, (dhi, dlo, ihi, ilo)), mask, g, gt, *first)

    def as_rows(array):
        return jnp.transpose(array.reshape(SLAB, C, NY, PLANE), (1, 2, 0, 3)).reshape(ROWS, PLANE)

    def as_planes(rows):
        return jnp.transpose(rows.reshape(C, NY, SLAB, PLANE), (2, 0, 1, 3)).reshape(1, SLAB, C, CELLS)

    def point(values, transposed, *bias):
        return pl.pallas_call(
            functools.partial(point_kernel, transposed),
            out_shape=[rows_out[1], jax.ShapeDtypeStruct((8, 128), F32)],
            compiler_params=params(24),
            cost_estimate=cost(4),
            name="point_in" if transposed else "point_up",
        )(values, point_weight, *bias)

    field_rows = as_rows(fields)
    sems = pltpu.SemaphoreType.DMA
    sent = pl.pallas_call(
        forward_kernel,
        in_specs=[pinned()] * 3,
        out_shape=slab_out,
        scratch_shapes=[
            pltpu.VMEM((ROWS, 128), BF16), pltpu.VMEM(ytab.shape, BF16), pltpu.VMEM(ztab.shape, BF16),
            planes, sems((STEPS + 2,)),
        ],
        compiler_params=params(56),
        cost_estimate=cost(3),
        name="slab_in",
    )(field_rows, ytab, ztab)
    mixed, spec_in = owner(exchange(sent.reshape(OWNERS, 32, 128)), False)
    local, _ = point(field_rows, True, point_bias[None, :])
    activated, upstream, sent = pl.pallas_call(
        middle_kernel,
        in_specs=[whole(flat), pinned(), pinned()] + table_specs + inverse_specs,
        out_specs=[pinned(), pinned(), whole(flat)],
        out_shape=rows_out + [slab_out],
        scratch_shapes=[pltpu.VMEM((ROWS, 128), dtype) for dtype in (F32, BF16, BF16, F32)]
        + [planes, planes, pltpu.VMEM((PAIR_ROWS, 256), F32)]
        + [pltpu.VMEM((PAIR_ROWS, 256), BF16)] * 2
        + [sems((4 * STEPS,))],
        compiler_params=params(52),
        cost_estimate=cost(8),
        name="slab_mid",
    )(exchange(mixed).reshape(flat), local, as_rows(cotangent), ytab, ztab, ytab_t, ztab_k)
    local, token = point(upstream, False)
    back, *sends = owner(exchange(sent.reshape(OWNERS, 32, 128)), True, spec_in, token)
    grad_input, done = pl.pallas_call(
        last_kernel,
        in_specs=[whole(flat), pinned()] + inverse_specs,
        out_specs=[pinned(), whole((8, 128))],
        out_shape=[rows_out[0], jax.ShapeDtypeStruct((8, 128), F32)],
        scratch_shapes=[pltpu.VMEM((ROWS, 128), dtype) for dtype in (F32, BF16)] + [planes, sems((2 * STEPS,))],
        compiler_params=params(52),
        cost_estimate=cost(20),
        name="slab_out",
    )(exchange(back).reshape(flat), local, ytab_t, ztab_k)

    def swap(block, bits):
        return lax.ppermute(block, "sample", [(s, s ^ bits) for s in range(SAMPLES)])

    far = swap(sends[4], 4)
    near = [swap(jnp.stack([sends[d], far[d]]), d) for d in range(1, 4)]
    grad_spectral = pl.pallas_call(
        weight_kernel,
        out_shape=jax.ShapeDtypeStruct((2 * C * C, BLOCK_MODES), F32),
        scratch_shapes=[pltpu.VMEM((SAMPLES, 2 * C, 128), F32)],
        compiler_params=params(8),
        cost_estimate=cost(1),
        name="weight_grad",
    )(sends[0], far, *near, done)
    grad_spectral = jnp.transpose(grad_spectral.reshape(C, C, 2, BLOCK_MODES), (2, 0, 1, 3))
    return as_planes(activated), as_planes(grad_input), grad_spectral


def solution(mesh):
    return jax.shard_map(
        shards,
        mesh=mesh,
        in_specs=(
            P("sample", "space", None, None),
            P("sample", "space", None, None),
            P(None, None, None, "space"),
            P(),
            P(),
        ),
        out_specs=(
            P("sample", "space", None, None),
            P("sample", "space", None, None),
            P(None, None, None, ("space", "sample")),
        ),
        check_vma=False,
    )
```

```python
import functools
import math

import jax
import jax.numpy as jnp
import ml_dtypes
import numpy as np
from jax import lax
from jax.experimental import pallas as pl
from jax.experimental.pallas import tpu as pltpu
from jax.sharding import PartitionSpec as P

NX, NY, NZ, NT = 64, 64, 32, 4
MX, MY, MZ, MT = 12, 12, 8, 4
C = 20
CP = 24
PLANE = NZ * NT
CELLS = NY * PLANE
KEPT_ROWS = C * MY
SLAB = 4
OWNERS = 16
SAMPLES = 8
BLOCK_MODES = 36
PAIRS = C // 2
CHUNK = 64
STEPS = C // 4
FAR = 1
NEAR = (0, 2, 4, 6)
ROWS = C * SLAB * NY
QUAD_ROWS = 4 * SLAB * NY
LAST_SINE = (12, 0)
CELL_ROWS = SLAB * NY
MIX = 16
VOLUME = NX * NY * NZ * NT
F32, BF16 = jnp.float32, jnp.bfloat16
MIB = 1024 * 1024


def signed(index, modes):
    return np.where(index < modes // 2, index, index - modes)


def hi_lo(table):
    hi = table.astype(np.float32).astype(ml_dtypes.bfloat16)
    lo = (table - hi.astype(np.float64)).astype(np.float32).astype(ml_dtypes.bfloat16)
    return hi, lo


def y_table():
    angle = 2 * np.pi * np.arange(NY) / NY
    rows = np.zeros((2, 16, NY))
    for parity in range(2):
        for k in range(7):
            rows[parity, 4 * parity + k] = np.cos(k * angle)
        for k in range(1, 6):
            rows[parity, 4 * parity + 6 + k] = -np.sin(k * angle)
        rows[parity, LAST_SINE[parity]] = np.sin(6 * angle)
    return np.einsum("prv,xz->pxrvz", rows, np.eye(SLAB)).reshape(2, 16 * SLAB, NY * SLAB)


def plane_table():
    z = np.arange(PLANE) // NT
    t = np.arange(PLANE) % NT
    rows = []
    for ql in range(2):
        q = 2 * np.arange(OWNERS) + ql
        fz = signed(q // MT, MZ)[:, None]
        ft = signed(q % MT, MT)[:, None]
        phase = (fz * z * NT + ft * t * NZ) % PLANE
        theta = 2 * np.pi * phase / PLANE
        rows.append(np.concatenate([np.cos(theta), np.sin(theta)], axis=1))
        rows.append(np.concatenate([-np.sin(theta), np.cos(theta)], axis=1))
    return np.concatenate(rows, axis=0)


def x_table(ql):
    lane = np.arange(256) + 128 * ql
    f = signed(lane % MX, MX)[None, :]
    theta = 2 * np.pi * ((f * np.arange(NX)[:, None]) % NX) / NX
    cos, sin = np.cos(theta), np.sin(theta)
    rows = [np.concatenate([cos, -sin], axis=1), np.concatenate([sin, cos], axis=1)]
    return np.stack(rows, axis=1).reshape(2 * NX, 512)


def mode_mask():
    fold = np.zeros((MY, MY), np.float32)
    fold[0, 0] = fold[6, 6] = 1.0
    for k in range(1, 6):
        fold[k, k] = fold[k, MY - k] = fold[6 + k, k] = 1.0
        fold[6 + k, MY - k] = -1.0
    mask = np.zeros((2, 24, 512), np.float32)
    for ql in range(2):
        lane = np.arange(256) + 128 * ql
        code = np.where(lane < 288, lane // MX, -1)
        here = code // MY == ql
        half = np.where(here[None, :], fold[np.arange(24) % MY][:, code % MY], 0.0)
        mask[ql] = np.concatenate([half, half], axis=1)
    return mask


def group_table():
    g = np.zeros((CP, KEPT_ROWS), np.float32)
    for c in range(C):
        g[c, c * MY : (c + 1) * MY] = 1.0
    return g


def split(value):
    hi = value.astype(BF16)
    return hi, (value - hi.astype(F32)).astype(BF16)


def dot(a, b):
    return lax.dot_general(a, b, (((1,), (0,)), ((), ())), preferred_element_type=F32)


def dot_tn(a, b):
    return lax.dot_general(a, b, (((0,), (0,)), ((), ())), preferred_element_type=F32)


def dot_nt(a, b):
    return lax.dot_general(a, b, (((1,), (1,)), ((), ())), preferred_element_type=F32)


def folded_rows(parity):
    return lax.broadcasted_iota(jnp.int32, (16, 128), 0) - 4 * parity


def forward_y(quad, cells, ytab, u_ref):
    for parity in range(2):
        first = 4 * quad + parity
        left, right = cells(first), cells(first + 2)
        table = ytab[parity]
        u = dot(table, jnp.concatenate([left[0], right[0]], axis=1))
        u = u[:64] + u[64:]
        if len(left) > 1:
            u = u + dot(table[:64], jnp.concatenate([left[1], right[1]], axis=1))
        k = folded_rows(parity)
        kept = slice(4 * parity, 4 * parity + MY)
        for side in range(2):
            at = (first + 2 * side) * MY
            for x in range(SLAB):
                group = u[x * 16 : (x + 1) * 16, side * 128 : (side + 1) * 128]
                sine = group[LAST_SINE[parity] : LAST_SINE[parity] + 1]
                real = jnp.where(k <= 6, group, 0.0)
                imag = jnp.where(k >= 7, group, jnp.where(k == 6, sine, 0.0))
                u_ref[x, at : at + MY, :128] = real[kept]
                u_ref[x, at : at + MY, 128:] = imag[kept]


def forward_plane(u_ref, ztab, out_ref):
    for x in range(SLAB):
        u_ref[x, KEPT_ROWS:, :] = jnp.zeros((256 - KEPT_ROWS, 256), F32)
        hi, lo = split(u_ref[x])
        both = dot_nt(ztab[...], hi)
        out = both[:64] + both[64:] + dot_nt(ztab[:64], lo)
        for ql in range(2):
            for reim in range(2):
                at = (ql * 2 + reim) * 16
                for half in range(2):
                    start = (ql * 2 + half) * 8 + x * 2 + reim
                    out_ref[pl.ds(start, OWNERS, stride=32), :] = out[at : at + 16, half * 128 : (half + 1) * 128]


def inverse_plane(recv_ref, ztab_k, h_ref):
    for x in range(SLAB):
        parts = []
        for ql in range(2):
            for reim in range(2):
                halves = [
                    recv_ref[pl.ds((ql * 2 + half) * 8 + x * 2 + reim, OWNERS, stride=32), :] for half in range(2)
                ]
                parts.append(jnp.concatenate(halves, axis=1))
        hi, lo = split(jnp.concatenate(parts, axis=0))
        h_ref[x] = dot_tn(jnp.concatenate([hi, lo, hi], axis=0), ztab_k[...])


def inverse_y(quad, h_ref, ytab_t):
    out = [None] * 4
    for parity in range(2):
        k = folded_rows(parity)
        last = LAST_SINE[parity] - 4 * parity
        sides = []
        for side in range(2):
            at = (4 * quad + parity + 2 * side) * MY - 4 * parity
            groups = []
            for x in range(SLAB):
                imag = h_ref[x, at : at + 16, 128:]
                sine = imag[4 * parity + 6 : 4 * parity + 7]
                group = jnp.where(k <= 6, h_ref[x, at : at + 16, :128], imag)
                groups.append(jnp.where(k == last, sine, group))
            sides.append(jnp.concatenate(groups, axis=0))
        hi, lo = split(jnp.concatenate(sides, axis=1))
        both = dot(ytab_t[parity], jnp.concatenate([hi, lo, hi], axis=0))
        out[parity], out[parity + 2] = both[:, :128], both[:, 128:]
    return out


def quad_rows(quad):
    return pl.ds(quad * QUAD_ROWS, QUAD_ROWS)


def fetch(source, target, sems, first):
    copies = [
        pltpu.make_async_copy(source.at[quad_rows(q)], target.at[quad_rows(q)], sems.at[first + q])
        for q in range(STEPS)
    ]
    return copies


def forward_kernel(x_hbm, ytab_hbm, ztab_hbm, out_ref, x_ref, ytab, ztab, u_ref, sems):
    tables = [
        pltpu.make_async_copy(ytab_hbm, ytab, sems.at[STEPS]),
        pltpu.make_async_copy(ztab_hbm, ztab, sems.at[STEPS + 1]),
    ]
    copies = fetch(x_hbm, x_ref, sems, 0)
    for copy in [copies[0], tables[0]] + copies[1:] + [tables[1]]:
        copy.start()
    tables[0].wait()
    for quad in range(STEPS):
        copies[quad].wait()
        forward_y(quad, lambda c: [x_ref[c * CELL_ROWS : (c + 1) * CELL_ROWS, :]], ytab, u_ref)
    tables[1].wait()
    forward_plane(u_ref, ztab, out_ref)


def middle_kernel(
    recv_ref, local_hbm, cot_hbm, ytab, ztab, ytab_t, ztab_k,
    act_hbm, up_hbm, out_ref,
    local_ref, cot_ref, act_ref, up_ref, h_ref, u_ref, pre_ref, hi_ref, lo_ref, sems,
):
    local_copies = fetch(local_hbm, local_ref, sems, 0)
    cot_copies = fetch(cot_hbm, cot_ref, sems, STEPS)
    for pair in zip(local_copies, cot_copies):
        for copy in pair:
            copy.start()
    stores = []
    inverse_plane(recv_ref, ztab_k, h_ref)
    for quad in range(STEPS):
        for k, block in enumerate(inverse_y(quad, h_ref, ytab_t)):
            pre_ref[k * CELL_ROWS : (k + 1) * CELL_ROWS, :] = block
        local_copies[quad].wait()
        cot_copies[quad].wait()
        for i in range(QUAD_ROWS // CHUNK):
            near = slice(i * CHUNK, (i + 1) * CHUNK)
            rows = slice(quad * QUAD_ROWS + i * CHUNK, quad * QUAD_ROWS + (i + 1) * CHUNK)
            pre = pre_ref[near, :] + local_ref[rows, :]
            cdf = 0.5 * (1.0 + lax.erf(pre * (1.0 / math.sqrt(2.0))))
            slope = cdf + pre * jnp.exp(-0.5 * pre * pre) * (1.0 / math.sqrt(2.0 * math.pi))
            act_ref[rows, :] = (pre * cdf).astype(BF16)
            up = cot_ref[rows, :].astype(F32) * slope
            up_ref[rows, :] = up
            hi_ref[near, :], lo_ref[near, :] = split(up)
        for k, (source, target) in enumerate(((act_ref, act_hbm), (up_ref, up_hbm))):
            store = pltpu.make_async_copy(
                source.at[quad_rows(quad)], target.at[quad_rows(quad)], sems.at[(2 + k) * STEPS + quad]
            )
            store.start()
            stores.append(store)
        def parts(c):
            rows = slice((c - 4 * quad) * CELL_ROWS, (c - 4 * quad + 1) * CELL_ROWS)
            return [hi_ref[rows, :], lo_ref[rows, :]]

        forward_y(quad, parts, ytab, u_ref)
    forward_plane(u_ref, ztab, out_ref)
    for store in stores:
        store.wait()


def weight_kernel(own_ref, far_ref, near1_ref, near2_ref, near3_ref, _, grad_ref, a_ref):
    near_refs = [near1_ref, near2_ref, near3_ref]
    even = lax.broadcasted_iota(jnp.int32, (2 * C, 128), 0) % 2 == 0
    terms = []
    for s, ref in enumerate([own_ref, far_ref.at[0]] + [ref.at[k] for ref in near_refs for k in range(2)]):
        block = ref[...]
        a_ref[s] = block
        b = pltpu.roll(block, 64, 1)
        below, above = pltpu.roll(b, 2 * C - 1, 0), pltpu.roll(b, 1, 0)
        terms.append((b, jnp.where(even, below, -above)))
    for c in range(C):
        total = jnp.zeros((2 * C, 128), F32)
        for s, (b, swapped) in enumerate(terms):
            total = total + (a_ref[s, 2 * c : 2 * c + 1, :] * b + a_ref[s, 2 * c + 1 : 2 * c + 2, :] * swapped)
        grad_ref[c * 2 * C : (c + 1) * 2 * C, :] = total[:, :BLOCK_MODES]


def last_kernel(recv_ref, local_hbm, ytab_t, ztab_k, out_hbm, token_ref, local_ref, out_ref, h_ref, sems):
    token_ref[...] = jnp.zeros_like(token_ref)
    local_copies = fetch(local_hbm, local_ref, sems, 0)
    for copy in local_copies:
        copy.start()
    stores = []
    inverse_plane(recv_ref, ztab_k, h_ref)
    for quad in range(STEPS):
        spectral = inverse_y(quad, h_ref, ytab_t)
        local_copies[quad].wait()
        for k in range(4):
            at = (4 * quad + k) * CELL_ROWS
            rows = slice(at, at + CELL_ROWS)
            out_ref[rows, :] = (spectral[k] + local_ref[rows, :]).astype(BF16)
        store = pltpu.make_async_copy(
            out_ref.at[quad_rows(quad)], out_hbm.at[quad_rows(quad)], sems.at[STEPS + quad]
        )
        store.start()
        stores.append(store)
    for store in stores:
        store.wait()


def point_kernel(transposed, x_ref, w_ref, *rest):
    bias_ref, out_ref, token_ref = rest if len(rest) == 3 else (None, *rest)
    token_ref[...] = jnp.zeros_like(token_ref)
    size = C * MIX
    row = lax.broadcasted_iota(jnp.int32, (size, C), 0)
    spread = (row // MIX == lax.broadcasted_iota(jnp.int32, (size, C), 1)).astype(F32)
    offset = jnp.sum(spread * bias_ref[...], axis=1, keepdims=True) if bias_ref is not None else 0.0
    spread = spread.astype(BF16)
    wide = (dot_nt if transposed else dot)(spread, w_ref[...]).astype(BF16)
    wide = dot_nt(wide, spread)
    row = lax.broadcasted_iota(jnp.int32, (size, size), 0)
    column = lax.broadcasted_iota(jnp.int32, (size, size), 1)
    wide = jnp.where(row % MIX == column % MIX, wide, 0.0).astype(BF16)
    for block in range(SLAB * NY // (2 * MIX)):
        sides = []
        for side in range(2):
            at = (2 * block + side) * MIX
            sides.append(
                jnp.concatenate([x_ref[c * SLAB * NY + at : c * SLAB * NY + at + MIX, :] for c in range(C)], axis=0)
            )
        both = jnp.concatenate(sides, axis=1)
        if both.dtype == BF16:
            out = dot(wide, both)
        else:
            hi, lo = split(both)
            out = dot(wide, hi) + dot(wide, lo)
        out = out + offset
        for side in range(2):
            at = (2 * block + side) * MIX
            for c in range(C):
                out_ref[c * SLAB * NY + at : c * SLAB * NY + at + MIX, :] = out[
                    c * MIX : (c + 1) * MIX, side * 128 : (side + 1) * 128
                ]


def owner_kernel(adjoint, s_ref, w_hbm, xhi, xlo, mask_ref, g_ref, *rest):
    *rest, w_ref, w_sem = rest
    fetch_w = pltpu.make_async_copy(w_hbm, w_ref, w_sem)
    fetch_w.start()
    if adjoint:
        first_ref, _, out_ref, *send_refs = rest[:8]
        f_ref, m_ref, turn_ref, b_ref = rest[8:]
        send_refs = send_refs[:4] + [send_refs[4].at[k] for k in range(4)]
    else:
        out_ref, spec_hbm, f_ref, m_ref, turn_ref, spec_ref, sem = rest
        store = pltpu.make_async_copy(spec_ref, spec_hbm, sem)
    g = g_ref[...]
    halves = []
    for ql in range(2):
        tiles = [s_ref[:, t * 8 : (t + 1) * 8, :].reshape(128, 128) for t in (2 * ql, 2 * ql + 1)]
        hi, lo = split(jnp.concatenate(tiles, axis=1))
        top = xhi[ql]
        rep = dot_tn(jnp.concatenate([hi, lo], axis=0), jnp.concatenate([top, top], axis=0)) + dot_tn(hi, xlo[ql])
        rep = rep[:KEPT_ROWS].reshape(PAIRS, 24, 512) * mask_ref[ql][None]
        hi, lo = split(rep.reshape(KEPT_ROWS, 512))
        halves.append(dot(g, hi) + dot(g, lo))
    for reim in range(2):
        a = halves[0][:, reim * 256 : (reim + 1) * 256]
        b = halves[1][:, reim * 256 : (reim + 1) * 256]
        joined = jnp.concatenate([a[:, :128], a[:, 128:] + b[:, :128], b[:, 128:]], axis=1)
        f_ref[reim] = joined * (1.0 / VOLUME) if adjoint else joined
    for reim in range(2):
        for t in range(3):
            turn_ref[t, pl.ds(reim, CP, stride=2), :] = f_ref[reim, :, t * 128 : (t + 1) * 128]
    turned = jnp.concatenate([turn_ref[t, : 2 * C, :] for t in range(3)], axis=1)
    for j in range(SAMPLES):
        block = turned[:, j * BLOCK_MODES : (j + 1) * BLOCK_MODES]
        if adjoint:
            b_ref[j, :, 64 : 64 + BLOCK_MODES] = block
            b_ref[j, :, :BLOCK_MODES] = first_ref[j, :, :BLOCK_MODES]
        else:
            spec_ref[j, :, :BLOCK_MODES] = block
    if adjoint:
        me = lax.axis_index("sample")
        for d in range(SAMPLES):
            send_refs[d][...] = b_ref[jnp.bitwise_xor(me, NEAR[d % 4] + FAR * (d // 4))]
    else:
        store.start()
    m_ref[...] = jnp.zeros_like(m_ref)
    fetch_w.wait()
    if adjoint:
        fr, fi = f_ref[0, :C, :288], f_ref[1, :C, :288]
        for c in range(C):
            wr, wi = w_ref[c].astype(F32), w_ref[C + c].astype(F32)
            m_ref[0, c : c + 1, :288] = jnp.sum(wr * fr + wi * fi, axis=0, keepdims=True)
            m_ref[1, c : c + 1, :288] = jnp.sum(wr * fi - wi * fr, axis=0, keepdims=True)
    else:
        mr = jnp.zeros((C, 288), F32)
        mi = jnp.zeros((C, 288), F32)
        for c in range(C):
            wr, wi = w_ref[c].astype(F32), w_ref[C + c].astype(F32)
            fr, fi = f_ref[0, c : c + 1, :288], f_ref[1, c : c + 1, :288]
            mr = mr + (wr * fr - wi * fi)
            mi = mi + (wr * fi + wi * fr)
        m_ref[0, :C, :288] = mr * (1.0 / VOLUME)
        m_ref[1, :C, :288] = mi * (1.0 / VOLUME)
    upper = lax.broadcasted_iota(jnp.int32, (24, 256), 0) < MY
    for ql in range(2):
        lanes = slice(ql * 128, ql * 128 + 256)
        mask = mask_ref[ql]
        rows = []
        for c in range(0, C, 2):
            pair = []
            for reim in range(2):
                even, odd = m_ref[reim, c : c + 1, lanes], m_ref[reim, c + 1 : c + 2, lanes]
                pair.append(jnp.where(upper, even, odd))
            rows.append(jnp.concatenate(pair, axis=1) * mask)
        rows.append(jnp.zeros((256 - KEPT_ROWS, 512), F32))
        hi, lo = split(jnp.concatenate(rows, axis=0))
        out = dot_nt(xhi[ql], hi) + dot_nt(xhi[ql], lo) + dot_nt(xlo[ql], hi)
        for half in range(2):
            t = 2 * ql + half
            out_ref[:, t * 8 : (t + 1) * 8, :] = out[:, half * 128 : (half + 1) * 128].reshape(OWNERS, 8, 128)
    if not adjoint:
        store.wait()


def whole(shape):
    return pl.BlockSpec(shape, lambda *_: (0,) * len(shape))


def pinned():
    return pl.BlockSpec(memory_space=pltpu.HBM)


def params(limit):
    return pltpu.CompilerParams(vmem_limit_bytes=int(limit * MIB))


def cost(us):
    return pl.CostEstimate(flops=int(us * 4e8), bytes_accessed=int(us * 3e6), transcendentals=0)


def exchange(block):
    return lax.all_to_all(block, "space", split_axis=0, concat_axis=0, tiled=True)


def shards(fields, cotangent, spectral_weight, point_weight, point_bias):
    yhi, ylo = hi_lo(y_table())
    zhi, zlo = hi_lo(plane_table())
    ytab = jnp.asarray(np.concatenate([yhi, ylo], axis=1))
    ztab = jnp.asarray(np.concatenate([zhi, zlo], axis=0))
    yhi_t, ylo_t = (np.swapaxes(t, 1, 2) for t in (yhi, ylo))
    ytab_t = jnp.asarray(np.concatenate([yhi_t, yhi_t, ylo_t], axis=2))
    ztab_k = jnp.asarray(np.concatenate([zhi, zhi, zlo], axis=0))
    mask = jnp.asarray(mode_mask())
    g = jnp.asarray(group_table().astype(ml_dtypes.bfloat16))
    xhi, xlo = map(jnp.asarray, hi_lo(np.stack([x_table(ql) for ql in range(2)])))
    flat = (OWNERS * 32, 128)
    slab_out = jax.ShapeDtypeStruct(flat, F32)
    owned_out = jax.ShapeDtypeStruct((OWNERS, 32, 128), F32)
    rows_out = [jax.ShapeDtypeStruct((ROWS, 128), dtype) for dtype in (BF16, F32)]
    table_specs = [whole(ytab.shape), whole(ztab.shape)]
    inverse_specs = [whole(ytab_t.shape), whole(ztab_k.shape)]
    planes = pltpu.VMEM((SLAB, 256, 256), F32)

    def owner(received, adjoint, *first):
        weights = spectral_weight.reshape(2 * C, C, 288)
        if adjoint:
            spec_shapes = [(2 * C, 128)] * 4 + [(4, 2 * C, 128)]
        else:
            spec_shapes = [(SAMPLES, 2 * C, 128)]
        scratch = [pltpu.VMEM((2, CP, 384), F32), pltpu.VMEM((2, CP, 384), F32), pltpu.VMEM((3, 2 * CP, 128), F32)]
        scratch.append(pltpu.VMEM((SAMPLES, 2 * C, 128), F32))
        operands = [received, weights, xhi, xlo, mask, g, *first]
        in_specs = [pinned() if k == 1 else whole(o.shape) for k, o in enumerate(operands)]
        if not adjoint:
            scratch.append(pltpu.SemaphoreType.DMA)
        return pl.pallas_call(
            functools.partial(owner_kernel, adjoint),
            out_shape=[owned_out] + [jax.ShapeDtypeStruct(shape, F32) for shape in spec_shapes],
            in_specs=in_specs,
            scratch_shapes=scratch + [pltpu.VMEM((2 * C, C, 288), BF16), pltpu.SemaphoreType.DMA],
            **({} if adjoint else {"out_specs": [whole(owned_out.shape), pinned()]}),
            compiler_params=params(52),
            cost_estimate=cost(3),
            name="owner_up" if adjoint else "owner_in",
        )(*operands)

    def as_rows(array):
        return jnp.transpose(array.reshape(SLAB, C, NY, PLANE), (1, 2, 0, 3)).reshape(ROWS, PLANE)

    def as_planes(rows):
        return jnp.transpose(rows.reshape(C, NY, SLAB, PLANE), (2, 0, 1, 3)).reshape(1, SLAB, C, CELLS)

    def point(values, transposed, *bias):
        return pl.pallas_call(
            functools.partial(point_kernel, transposed),
            out_shape=[rows_out[1], jax.ShapeDtypeStruct((8, 128), F32)],
            compiler_params=params(24),
            cost_estimate=cost(4),
            name="point_in" if transposed else "point_up",
        )(values, point_weight, *bias)

    field_rows = as_rows(fields)
    sems = pltpu.SemaphoreType.DMA
    sent = pl.pallas_call(
        forward_kernel,
        in_specs=[pinned()] * 3,
        out_shape=slab_out,
        scratch_shapes=[
            pltpu.VMEM((ROWS, 128), BF16), pltpu.VMEM(ytab.shape, BF16), pltpu.VMEM(ztab.shape, BF16),
            planes, sems((STEPS + 2,)),
        ],
        compiler_params=params(56),
        cost_estimate=cost(3),
        name="slab_in",
    )(field_rows, ytab, ztab)
    mixed, spec_in = owner(exchange(sent.reshape(OWNERS, 32, 128)), False)
    local, _ = point(field_rows, True, point_bias[None, :])
    activated, upstream, sent = pl.pallas_call(
        middle_kernel,
        in_specs=[whole(flat), pinned(), pinned()] + table_specs + inverse_specs,
        out_specs=[pinned(), pinned(), whole(flat)],
        out_shape=rows_out + [slab_out],
        scratch_shapes=[pltpu.VMEM((ROWS, 128), dtype) for dtype in (F32, BF16, BF16, F32)]
        + [planes, planes, pltpu.VMEM((QUAD_ROWS, 128), F32)]
        + [pltpu.VMEM((QUAD_ROWS, 128), BF16)] * 2
        + [sems((4 * STEPS,))],
        compiler_params=params(52),
        cost_estimate=cost(8),
        name="slab_mid",
    )(exchange(mixed).reshape(flat), local, as_rows(cotangent), ytab, ztab, ytab_t, ztab_k)
    local, token = point(upstream, False)
    back, *sends = owner(exchange(sent.reshape(OWNERS, 32, 128)), True, spec_in, token)
    def swap(block, bits):
        return lax.ppermute(block, "sample", [(s, s ^ bits) for s in range(SAMPLES)])

    far = swap(sends[4], FAR)
    near = [swap(jnp.stack([sends[k], far[k]]), NEAR[k]) for k in range(1, 4)]
    grad_input, done = pl.pallas_call(
        last_kernel,
        in_specs=[whole(flat), pinned()] + inverse_specs,
        out_specs=[pinned(), whole((8, 128))],
        out_shape=[rows_out[0], jax.ShapeDtypeStruct((8, 128), F32)],
        scratch_shapes=[pltpu.VMEM((ROWS, 128), dtype) for dtype in (F32, BF16)] + [planes, sems((2 * STEPS,))],
        compiler_params=params(52),
        cost_estimate=cost(20),
        name="slab_out",
    )(exchange(back).reshape(flat), local, ytab_t, ztab_k)
    grad_spectral = pl.pallas_call(
        weight_kernel,
        out_shape=jax.ShapeDtypeStruct((2 * C * C, BLOCK_MODES), F32),
        scratch_shapes=[pltpu.VMEM((SAMPLES, 2 * C, 128), F32)],
        compiler_params=params(8),
        cost_estimate=cost(1),
        name="weight_grad",
    )(sends[0], far, *near, done)
    grad_spectral = jnp.transpose(grad_spectral.reshape(C, C, 2, BLOCK_MODES), (2, 0, 1, 3))
    return as_planes(activated), as_planes(grad_input), grad_spectral


def solution(mesh):
    return jax.shard_map(
        shards,
        mesh=mesh,
        in_specs=(
            P("sample", "space", None, None),
            P("sample", "space", None, None),
            P(None, None, None, "space"),
            P(),
            P(),
        ),
        out_specs=(
            P("sample", "space", None, None),
            P("sample", "space", None, None),
            P(None, None, None, ("space", "sample")),
        ),
        check_vma=False,
    )
```

```python
import functools
import math

import jax
import jax.numpy as jnp
import ml_dtypes
import numpy as np
from jax import lax
from jax.experimental import pallas as pl
from jax.experimental.pallas import tpu as pltpu
from jax.sharding import PartitionSpec as P

NX, NY, NZ, NT = 64, 64, 32, 4
MX, MY, MZ, MT = 12, 12, 8, 4
C = 20
CP = 24
PLANE = NZ * NT
CELLS = NY * PLANE
KEPT_ROWS = C * MY
SLAB = 4
OWNERS = 16
SAMPLES = 8
BLOCK_MODES = 36
PAIRS = C // 2
CHUNK = 64
STEPS = C // 4
FAR = 1
NEAR = (0, 2, 4, 6)
ROWS = C * SLAB * NY
QUAD_ROWS = 4 * SLAB * NY
LAST_SINE = (12, 0)
CELL_ROWS = SLAB * NY
MIX = 16
VOLUME = NX * NY * NZ * NT
F32, BF16 = jnp.float32, jnp.bfloat16
MIB = 1024 * 1024


def signed(index, modes):
    return np.where(index < modes // 2, index, index - modes)


def hi_lo(table):
    hi = table.astype(np.float32).astype(ml_dtypes.bfloat16)
    lo = (table - hi.astype(np.float64)).astype(np.float32).astype(ml_dtypes.bfloat16)
    return hi, lo


def y_table():
    angle = 2 * np.pi * np.arange(NY) / NY
    rows = np.zeros((2, 16, NY))
    for parity in range(2):
        for k in range(7):
            rows[parity, 4 * parity + k] = np.cos(k * angle)
        for k in range(1, 6):
            rows[parity, 4 * parity + 6 + k] = -np.sin(k * angle)
        rows[parity, LAST_SINE[parity]] = np.sin(6 * angle)
    return np.einsum("prv,xz->pxrvz", rows, np.eye(SLAB)).reshape(2, 16 * SLAB, NY * SLAB)


def plane_table():
    z = np.arange(PLANE) // NT
    t = np.arange(PLANE) % NT
    rows = []
    for ql in range(2):
        q = 2 * np.arange(OWNERS) + ql
        fz = signed(q // MT, MZ)[:, None]
        ft = signed(q % MT, MT)[:, None]
        phase = (fz * z * NT + ft * t * NZ) % PLANE
        theta = 2 * np.pi * phase / PLANE
        rows.append(np.concatenate([np.cos(theta), np.sin(theta)], axis=1))
        rows.append(np.concatenate([-np.sin(theta), np.cos(theta)], axis=1))
    return np.concatenate(rows, axis=0)


def x_table(ql):
    lane = np.arange(256) + 128 * ql
    f = signed(lane % MX, MX)[None, :]
    theta = 2 * np.pi * ((f * np.arange(NX)[:, None]) % NX) / NX
    cos, sin = np.cos(theta), np.sin(theta)
    rows = [np.concatenate([cos, -sin], axis=1), np.concatenate([sin, cos], axis=1)]
    return np.stack(rows, axis=1).reshape(2 * NX, 512)


def mode_mask():
    fold = np.zeros((MY, MY), np.float32)
    fold[0, 0] = fold[6, 6] = 1.0
    for k in range(1, 6):
        fold[k, k] = fold[k, MY - k] = fold[6 + k, k] = 1.0
        fold[6 + k, MY - k] = -1.0
    mask = np.zeros((2, 24, 512), np.float32)
    for ql in range(2):
        lane = np.arange(256) + 128 * ql
        code = np.where(lane < 288, lane // MX, -1)
        here = code // MY == ql
        half = np.where(here[None, :], fold[np.arange(24) % MY][:, code % MY], 0.0)
        mask[ql] = np.concatenate([half, half], axis=1)
    return mask


def group_table():
    g = np.zeros((CP, KEPT_ROWS), np.float32)
    for c in range(C):
        g[c, c * MY : (c + 1) * MY] = 1.0
    return g


def split(value):
    hi = value.astype(BF16)
    return hi, (value - hi.astype(F32)).astype(BF16)


def dot(a, b):
    return lax.dot_general(a, b, (((1,), (0,)), ((), ())), preferred_element_type=F32)


def dot_tn(a, b):
    return lax.dot_general(a, b, (((0,), (0,)), ((), ())), preferred_element_type=F32)


def dot_nt(a, b):
    return lax.dot_general(a, b, (((1,), (1,)), ((), ())), preferred_element_type=F32)


def folded_rows(parity):
    return lax.broadcasted_iota(jnp.int32, (16, 128), 0) - 4 * parity


def forward_y(quad, cells, ytab, u_ref):
    for parity in range(2):
        first = 4 * quad + parity
        left, right = cells(first), cells(first + 2)
        table = ytab[parity]
        u = dot(table, jnp.concatenate([left[0], right[0]], axis=1))
        u = u[:64] + u[64:]
        if len(left) > 1:
            u = u + dot(table[:64], jnp.concatenate([left[1], right[1]], axis=1))
        k = folded_rows(parity)
        kept = slice(4 * parity, 4 * parity + MY)
        for side in range(2):
            at = (first + 2 * side) * MY
            for x in range(SLAB):
                group = u[x * 16 : (x + 1) * 16, side * 128 : (side + 1) * 128]
                sine = group[LAST_SINE[parity] : LAST_SINE[parity] + 1]
                real = jnp.where(k <= 6, group, 0.0)
                imag = jnp.where(k >= 7, group, jnp.where(k == 6, sine, 0.0))
                u_ref[x, at : at + MY, :128] = real[kept]
                u_ref[x, at : at + MY, 128:] = imag[kept]


def forward_plane(u_ref, ztab, out_ref):
    for x in range(SLAB):
        u_ref[x, KEPT_ROWS:, :] = jnp.zeros((256 - KEPT_ROWS, 256), F32)
        hi, lo = split(u_ref[x])
        both = dot_nt(ztab[...], hi)
        out = both[:64] + both[64:] + dot_nt(ztab[:64], lo)
        for ql in range(2):
            for reim in range(2):
                at = (ql * 2 + reim) * 16
                for half in range(2):
                    start = (ql * 2 + half) * 8 + x * 2 + reim
                    out_ref[pl.ds(start, OWNERS, stride=32), :] = out[at : at + 16, half * 128 : (half + 1) * 128]


def inverse_plane(recv_ref, ztab_k, h_ref):
    for x in range(SLAB):
        parts = []
        for ql in range(2):
            for reim in range(2):
                halves = [
                    recv_ref[pl.ds((ql * 2 + half) * 8 + x * 2 + reim, OWNERS, stride=32), :] for half in range(2)
                ]
                parts.append(jnp.concatenate(halves, axis=1))
        hi, lo = split(jnp.concatenate(parts, axis=0))
        h_ref[x] = dot_tn(jnp.concatenate([hi, lo, hi], axis=0), ztab_k[...])


def inverse_y(quad, h_ref, ytab_t):
    out = [None] * 4
    for parity in range(2):
        k = folded_rows(parity)
        last = LAST_SINE[parity] - 4 * parity
        sides = []
        for side in range(2):
            at = (4 * quad + parity + 2 * side) * MY - 4 * parity
            groups = []
            for x in range(SLAB):
                imag = h_ref[x, at : at + 16, 128:]
                sine = imag[4 * parity + 6 : 4 * parity + 7]
                group = jnp.where(k <= 6, h_ref[x, at : at + 16, :128], imag)
                groups.append(jnp.where(k == last, sine, group))
            sides.append(jnp.concatenate(groups, axis=0))
        hi, lo = split(jnp.concatenate(sides, axis=1))
        both = dot(ytab_t[parity], jnp.concatenate([hi, lo, hi], axis=0))
        out[parity], out[parity + 2] = both[:, :128], both[:, 128:]
    return out


def quad_rows(quad):
    return pl.ds(quad * QUAD_ROWS, QUAD_ROWS)


def fetch(source, target, sems, first):
    copies = [
        pltpu.make_async_copy(source.at[quad_rows(q)], target.at[quad_rows(q)], sems.at[first + q])
        for q in range(STEPS)
    ]
    return copies


def forward_kernel(x_hbm, ytab_hbm, ztab_hbm, out_ref, x_ref, ytab, ztab, u_ref, sems):
    tables = [
        pltpu.make_async_copy(ytab_hbm, ytab, sems.at[STEPS]),
        pltpu.make_async_copy(ztab_hbm, ztab, sems.at[STEPS + 1]),
    ]
    copies = fetch(x_hbm, x_ref, sems, 0)
    for copy in [copies[0], tables[0]] + copies[1:] + [tables[1]]:
        copy.start()
    tables[0].wait()
    for quad in range(STEPS):
        copies[quad].wait()
        forward_y(quad, lambda c: [x_ref[c * CELL_ROWS : (c + 1) * CELL_ROWS, :]], ytab, u_ref)
    tables[1].wait()
    forward_plane(u_ref, ztab, out_ref)


def middle_kernel(
    recv_ref, local_hbm, cot_hbm, ytab, ztab, ytab_t, ztab_k,
    act_hbm, up_hbm, out_ref,
    local_ref, cot_ref, act_ref, up_ref, h_ref, u_ref, pre_ref, hi_ref, lo_ref, sems,
):
    local_copies = fetch(local_hbm, local_ref, sems, 0)
    cot_copies = fetch(cot_hbm, cot_ref, sems, STEPS)
    for pair in zip(local_copies, cot_copies):
        for copy in pair:
            copy.start()
    stores = []
    inverse_plane(recv_ref, ztab_k, h_ref)
    for quad in range(STEPS):
        for k, block in enumerate(inverse_y(quad, h_ref, ytab_t)):
            pre_ref[k * CELL_ROWS : (k + 1) * CELL_ROWS, :] = block
        local_copies[quad].wait()
        cot_copies[quad].wait()
        for i in range(QUAD_ROWS // CHUNK):
            near = slice(i * CHUNK, (i + 1) * CHUNK)
            rows = slice(quad * QUAD_ROWS + i * CHUNK, quad * QUAD_ROWS + (i + 1) * CHUNK)
            pre = pre_ref[near, :] + local_ref[rows, :]
            cdf = 0.5 * (1.0 + lax.erf(pre * (1.0 / math.sqrt(2.0))))
            slope = cdf + pre * jnp.exp(-0.5 * pre * pre) * (1.0 / math.sqrt(2.0 * math.pi))
            act_ref[rows, :] = (pre * cdf).astype(BF16)
            up = cot_ref[rows, :].astype(F32) * slope
            up_ref[rows, :] = up
            hi_ref[near, :], lo_ref[near, :] = split(up)
        for k, (source, target) in enumerate(((act_ref, act_hbm), (up_ref, up_hbm))):
            store = pltpu.make_async_copy(
                source.at[quad_rows(quad)], target.at[quad_rows(quad)], sems.at[(2 + k) * STEPS + quad]
            )
            store.start()
            stores.append(store)
        def parts(c):
            rows = slice((c - 4 * quad) * CELL_ROWS, (c - 4 * quad + 1) * CELL_ROWS)
            return [hi_ref[rows, :], lo_ref[rows, :]]

        forward_y(quad, parts, ytab, u_ref)
    forward_plane(u_ref, ztab, out_ref)
    for store in stores:
        store.wait()


def weight_kernel(own_ref, far_ref, near1_ref, near2_ref, near3_ref, _, grad_ref, a_ref):
    near_refs = [near1_ref, near2_ref, near3_ref]
    even = lax.broadcasted_iota(jnp.int32, (2 * C, 128), 0) % 2 == 0
    terms = []
    for s, ref in enumerate([own_ref, far_ref.at[0]] + [ref.at[k] for ref in near_refs for k in range(2)]):
        block = ref[...]
        a_ref[s] = block
        b = pltpu.roll(block, 64, 1)
        below, above = pltpu.roll(b, 2 * C - 1, 0), pltpu.roll(b, 1, 0)
        terms.append((b, jnp.where(even, below, -above)))
    for c in range(C):
        total = jnp.zeros((2 * C, 128), F32)
        for s, (b, swapped) in enumerate(terms):
            total = total + (a_ref[s, 2 * c : 2 * c + 1, :] * b + a_ref[s, 2 * c + 1 : 2 * c + 2, :] * swapped)
        grad_ref[c * 2 * C : (c + 1) * 2 * C, :] = total[:, :BLOCK_MODES]


def last_kernel(recv_ref, local_hbm, ytab_t, ztab_k, out_hbm, token_ref, local_ref, out_ref, h_ref, sems):
    token_ref[...] = jnp.zeros_like(token_ref)
    local_copies = fetch(local_hbm, local_ref, sems, 0)
    for copy in local_copies:
        copy.start()
    stores = []
    inverse_plane(recv_ref, ztab_k, h_ref)
    for quad in range(STEPS):
        spectral = inverse_y(quad, h_ref, ytab_t)
        local_copies[quad].wait()
        for k in range(4):
            at = (4 * quad + k) * CELL_ROWS
            rows = slice(at, at + CELL_ROWS)
            out_ref[rows, :] = (spectral[k] + local_ref[rows, :]).astype(BF16)
        store = pltpu.make_async_copy(
            out_ref.at[quad_rows(quad)], out_hbm.at[quad_rows(quad)], sems.at[STEPS + quad]
        )
        store.start()
        stores.append(store)
    for store in stores:
        store.wait()


def point_kernel(transposed, x_ref, w_ref, *rest):
    bias_ref, out_ref, token_ref = rest if len(rest) == 3 else (None, *rest)
    token_ref[...] = jnp.zeros_like(token_ref)
    size = C * MIX
    row = lax.broadcasted_iota(jnp.int32, (size, C), 0)
    spread = (row // MIX == lax.broadcasted_iota(jnp.int32, (size, C), 1)).astype(F32)
    offset = jnp.sum(spread * bias_ref[...], axis=1, keepdims=True) if bias_ref is not None else 0.0
    spread = spread.astype(BF16)
    wide = (dot_nt if transposed else dot)(spread, w_ref[...]).astype(BF16)
    wide = dot_nt(wide, spread)
    row = lax.broadcasted_iota(jnp.int32, (size, size), 0)
    column = lax.broadcasted_iota(jnp.int32, (size, size), 1)
    wide = jnp.where(row % MIX == column % MIX, wide, 0.0).astype(BF16)
    for block in range(SLAB * NY // (2 * MIX)):
        sides = []
        for side in range(2):
            at = (2 * block + side) * MIX
            sides.append(
                jnp.concatenate([x_ref[c * SLAB * NY + at : c * SLAB * NY + at + MIX, :] for c in range(C)], axis=0)
            )
        both = jnp.concatenate(sides, axis=1)
        if both.dtype == BF16:
            out = dot(wide, both)
        else:
            hi, lo = split(both)
            out = dot(wide, hi) + dot(wide, lo)
        out = out + offset
        for side in range(2):
            at = (2 * block + side) * MIX
            for c in range(C):
                out_ref[c * SLAB * NY + at : c * SLAB * NY + at + MIX, :] = out[
                    c * MIX : (c + 1) * MIX, side * 128 : (side + 1) * 128
                ]


def owner_kernel(adjoint, s_ref, w_hbm, xhi, xlo, mask_ref, g_ref, *rest):
    *rest, w_ref, w_sem, out_ref, out_sems = rest
    fetch_w = pltpu.make_async_copy(w_hbm, w_ref, w_sem)
    fetch_w.start()
    if adjoint:
        first_ref, _, out_hbm, *send_refs = rest[:8]
        f_ref, m_ref, turn_ref, b_ref = rest[8:]
        send_refs = send_refs[:4] + [send_refs[4].at[k] for k in range(4)]
    else:
        out_hbm, spec_hbm, f_ref, m_ref, turn_ref, spec_ref, sem = rest
        store = pltpu.make_async_copy(spec_ref, spec_hbm, sem)
    g = g_ref[...]
    halves = []
    for ql in range(2):
        tiles = [s_ref[:, t * 8 : (t + 1) * 8, :].reshape(128, 128) for t in (2 * ql, 2 * ql + 1)]
        hi, lo = split(jnp.concatenate(tiles, axis=1))
        top = xhi[ql]
        rep = dot_tn(jnp.concatenate([hi, lo], axis=0), jnp.concatenate([top, top], axis=0)) + dot_tn(hi, xlo[ql])
        rep = rep[:KEPT_ROWS].reshape(PAIRS, 24, 512) * mask_ref[ql][None]
        hi, lo = split(rep.reshape(KEPT_ROWS, 512))
        halves.append(dot(g, hi) + dot(g, lo))
    for reim in range(2):
        a = halves[0][:, reim * 256 : (reim + 1) * 256]
        b = halves[1][:, reim * 256 : (reim + 1) * 256]
        joined = jnp.concatenate([a[:, :128], a[:, 128:] + b[:, :128], b[:, 128:]], axis=1)
        f_ref[reim] = joined * (1.0 / VOLUME) if adjoint else joined
    for reim in range(2):
        for t in range(3):
            turn_ref[t, pl.ds(reim, CP, stride=2), :] = f_ref[reim, :, t * 128 : (t + 1) * 128]
    turned = jnp.concatenate([turn_ref[t, : 2 * C, :] for t in range(3)], axis=1)
    for j in range(SAMPLES):
        block = turned[:, j * BLOCK_MODES : (j + 1) * BLOCK_MODES]
        if adjoint:
            b_ref[j, :, 64 : 64 + BLOCK_MODES] = block
            b_ref[j, :, :BLOCK_MODES] = first_ref[j, :, :BLOCK_MODES]
        else:
            spec_ref[j, :, :BLOCK_MODES] = block
    if adjoint:
        me = lax.axis_index("sample")
        for d in range(SAMPLES):
            send_refs[d][...] = b_ref[jnp.bitwise_xor(me, NEAR[d % 4] + FAR * (d // 4))]
    else:
        store.start()
    m_ref[...] = jnp.zeros_like(m_ref)
    fetch_w.wait()
    if adjoint:
        fr, fi = f_ref[0, :C, :288], f_ref[1, :C, :288]
        for c in range(C):
            wr, wi = w_ref[c].astype(F32), w_ref[C + c].astype(F32)
            m_ref[0, c : c + 1, :288] = jnp.sum(wr * fr + wi * fi, axis=0, keepdims=True)
            m_ref[1, c : c + 1, :288] = jnp.sum(wr * fi - wi * fr, axis=0, keepdims=True)
    else:
        mr = jnp.zeros((C, 288), F32)
        mi = jnp.zeros((C, 288), F32)
        for c in range(C):
            wr, wi = w_ref[c].astype(F32), w_ref[C + c].astype(F32)
            fr, fi = f_ref[0, c : c + 1, :288], f_ref[1, c : c + 1, :288]
            mr = mr + (wr * fr - wi * fi)
            mi = mi + (wr * fi + wi * fr)
        m_ref[0, :C, :288] = mr * (1.0 / VOLUME)
        m_ref[1, :C, :288] = mi * (1.0 / VOLUME)
    sent = []
    upper = lax.broadcasted_iota(jnp.int32, (24, 256), 0) < MY
    for ql in range(2):
        lanes = slice(ql * 128, ql * 128 + 256)
        mask = mask_ref[ql]
        rows = []
        for c in range(0, C, 2):
            pair = []
            for reim in range(2):
                even, odd = m_ref[reim, c : c + 1, lanes], m_ref[reim, c + 1 : c + 2, lanes]
                pair.append(jnp.where(upper, even, odd))
            rows.append(jnp.concatenate(pair, axis=1) * mask)
        rows.append(jnp.zeros((256 - KEPT_ROWS, 512), F32))
        hi, lo = split(jnp.concatenate(rows, axis=0))
        both = dot_nt(jnp.concatenate([xhi[ql], xlo[ql]], axis=0), hi)
        out = both[:128] + both[128:] + dot_nt(xhi[ql], lo)
        for half in range(2):
            t = 2 * ql + half
            out_ref[:, t * 8 : (t + 1) * 8, :] = out[:, half * 128 : (half + 1) * 128].reshape(OWNERS, 8, 128)
        part = (slice(None), pl.ds(ql * 16, 16), slice(None))
        sent.append(pltpu.make_async_copy(out_ref.at[part], out_hbm.at[part], out_sems.at[ql]))
        sent[ql].start()
    for copy in sent:
        copy.wait()
    if not adjoint:
        store.wait()


def whole(shape):
    return pl.BlockSpec(shape, lambda *_: (0,) * len(shape))


def pinned():
    return pl.BlockSpec(memory_space=pltpu.HBM)


def params(limit):
    return pltpu.CompilerParams(vmem_limit_bytes=int(limit * MIB))


def cost(us):
    return pl.CostEstimate(flops=int(us * 4e8), bytes_accessed=int(us * 3e6), transcendentals=0)


def exchange(block):
    return lax.all_to_all(block, "space", split_axis=0, concat_axis=0, tiled=True)


def shards(fields, cotangent, spectral_weight, point_weight, point_bias):
    yhi, ylo = hi_lo(y_table())
    zhi, zlo = hi_lo(plane_table())
    ytab = jnp.asarray(np.concatenate([yhi, ylo], axis=1))
    ztab = jnp.asarray(np.concatenate([zhi, zlo], axis=0))
    yhi_t, ylo_t = (np.swapaxes(t, 1, 2) for t in (yhi, ylo))
    ytab_t = jnp.asarray(np.concatenate([yhi_t, yhi_t, ylo_t], axis=2))
    ztab_k = jnp.asarray(np.concatenate([zhi, zhi, zlo], axis=0))
    mask = jnp.asarray(mode_mask())
    g = jnp.asarray(group_table().astype(ml_dtypes.bfloat16))
    xhi, xlo = map(jnp.asarray, hi_lo(np.stack([x_table(ql) for ql in range(2)])))
    flat = (OWNERS * 32, 128)
    slab_out = jax.ShapeDtypeStruct(flat, F32)
    owned_out = jax.ShapeDtypeStruct((OWNERS, 32, 128), F32)
    rows_out = [jax.ShapeDtypeStruct((ROWS, 128), dtype) for dtype in (BF16, F32)]
    table_specs = [whole(ytab.shape), whole(ztab.shape)]
    inverse_specs = [whole(ytab_t.shape), whole(ztab_k.shape)]
    planes = pltpu.VMEM((SLAB, 256, 256), F32)

    def owner(received, adjoint, *first):
        weights = spectral_weight.reshape(2 * C, C, 288)
        if adjoint:
            spec_shapes = [(2 * C, 128)] * 4 + [(4, 2 * C, 128)]
        else:
            spec_shapes = [(SAMPLES, 2 * C, 128)]
        scratch = [pltpu.VMEM((2, CP, 384), F32), pltpu.VMEM((2, CP, 384), F32), pltpu.VMEM((3, 2 * CP, 128), F32)]
        scratch.append(pltpu.VMEM((SAMPLES, 2 * C, 128), F32))
        operands = [received, weights, xhi, xlo, mask, g, *first]
        in_specs = [pinned() if k == 1 else whole(o.shape) for k, o in enumerate(operands)]
        if not adjoint:
            scratch.append(pltpu.SemaphoreType.DMA)
        return pl.pallas_call(
            functools.partial(owner_kernel, adjoint),
            out_shape=[owned_out] + [jax.ShapeDtypeStruct(shape, F32) for shape in spec_shapes],
            in_specs=in_specs,
            scratch_shapes=scratch
            + [pltpu.VMEM((2 * C, C, 288), BF16), pltpu.SemaphoreType.DMA]
            + [pltpu.VMEM(owned_out.shape, F32), pltpu.SemaphoreType.DMA((2,))],
            out_specs=[pinned()] + (list(map(whole, spec_shapes)) if adjoint else [pinned()]),
            compiler_params=params(52),
            cost_estimate=cost(3),
            name="owner_up" if adjoint else "owner_in",
        )(*operands)

    def as_rows(array):
        return jnp.transpose(array.reshape(SLAB, C, NY, PLANE), (1, 2, 0, 3)).reshape(ROWS, PLANE)

    def as_planes(rows):
        return jnp.transpose(rows.reshape(C, NY, SLAB, PLANE), (2, 0, 1, 3)).reshape(1, SLAB, C, CELLS)

    def point(values, transposed, *bias):
        return pl.pallas_call(
            functools.partial(point_kernel, transposed),
            out_shape=[rows_out[1], jax.ShapeDtypeStruct((8, 128), F32)],
            compiler_params=params(24),
            cost_estimate=cost(4),
            name="point_in" if transposed else "point_up",
        )(values, point_weight, *bias)

    field_rows = as_rows(fields)
    sems = pltpu.SemaphoreType.DMA
    sent = pl.pallas_call(
        forward_kernel,
        in_specs=[pinned()] * 3,
        out_shape=slab_out,
        scratch_shapes=[
            pltpu.VMEM((ROWS, 128), BF16), pltpu.VMEM(ytab.shape, BF16), pltpu.VMEM(ztab.shape, BF16),
            planes, sems((STEPS + 2,)),
        ],
        compiler_params=params(56),
        cost_estimate=cost(3),
        name="slab_in",
    )(field_rows, ytab, ztab)
    mixed, spec_in = owner(exchange(sent.reshape(OWNERS, 32, 128)), False)
    local, _ = point(field_rows, True, point_bias[None, :])
    activated, upstream, sent = pl.pallas_call(
        middle_kernel,
        in_specs=[whole(flat), pinned(), pinned()] + table_specs + inverse_specs,
        out_specs=[pinned(), pinned(), whole(flat)],
        out_shape=rows_out + [slab_out],
        scratch_shapes=[pltpu.VMEM((ROWS, 128), dtype) for dtype in (F32, BF16, BF16, F32)]
        + [planes, planes, pltpu.VMEM((QUAD_ROWS, 128), F32)]
        + [pltpu.VMEM((QUAD_ROWS, 128), BF16)] * 2
        + [sems((4 * STEPS,))],
        compiler_params=params(52),
        cost_estimate=cost(8),
        name="slab_mid",
    )(exchange(mixed).reshape(flat), local, as_rows(cotangent), ytab, ztab, ytab_t, ztab_k)
    local, token = point(upstream, False)
    back, *sends = owner(exchange(sent.reshape(OWNERS, 32, 128)), True, spec_in, token)
    def swap(block, bits):
        return lax.ppermute(block, "sample", [(s, s ^ bits) for s in range(SAMPLES)])

    far = swap(sends[4], FAR)
    near = [swap(jnp.stack([sends[k], far[k]]), NEAR[k]) for k in range(1, 4)]
    grad_input, done = pl.pallas_call(
        last_kernel,
        in_specs=[whole(flat), pinned()] + inverse_specs,
        out_specs=[pinned(), whole((8, 128))],
        out_shape=[rows_out[0], jax.ShapeDtypeStruct((8, 128), F32)],
        scratch_shapes=[pltpu.VMEM((ROWS, 128), dtype) for dtype in (F32, BF16)] + [planes, sems((2 * STEPS,))],
        compiler_params=params(52),
        cost_estimate=cost(20),
        name="slab_out",
    )(exchange(back).reshape(flat), local, ytab_t, ztab_k)
    grad_spectral = pl.pallas_call(
        weight_kernel,
        out_shape=jax.ShapeDtypeStruct((2 * C * C, BLOCK_MODES), F32),
        scratch_shapes=[pltpu.VMEM((SAMPLES, 2 * C, 128), F32)],
        compiler_params=params(8),
        cost_estimate=cost(1),
        name="weight_grad",
    )(sends[0], far, *near, done)
    grad_spectral = jnp.transpose(grad_spectral.reshape(C, C, 2, BLOCK_MODES), (2, 0, 1, 3))
    return as_planes(activated), as_planes(grad_input), grad_spectral


def solution(mesh):
    return jax.shard_map(
        shards,
        mesh=mesh,
        in_specs=(
            P("sample", "space", None, None),
            P("sample", "space", None, None),
            P(None, None, None, "space"),
            P(),
            P(),
        ),
        out_specs=(
            P("sample", "space", None, None),
            P("sample", "space", None, None),
            P(None, None, None, ("space", "sample")),
        ),
        check_vma=False,
    )
```

```python
import functools
import math

import jax
import jax.numpy as jnp
import ml_dtypes
import numpy as np
from jax import lax
from jax.experimental import pallas as pl
from jax.experimental.pallas import tpu as pltpu
from jax.sharding import PartitionSpec as P

NX, NY, NZ, NT = 64, 64, 32, 4
MX, MY, MZ, MT = 12, 12, 8, 4
C = 20
CP = 24
PLANE = NZ * NT
CELLS = NY * PLANE
KEPT_ROWS = C * MY
SLAB = 4
OWNERS = 16
SAMPLES = 8
BLOCK_MODES = 36
PAIRS = C // 2
CHUNK = 64
STEPS = C // 4
AHEAD = 3
FAR = 1
NEAR = (0, 2, 4, 6)
ROWS = C * SLAB * NY
QUAD_ROWS = 4 * SLAB * NY
LAST_SINE = (12, 0)
CELL_ROWS = SLAB * NY
MIX = 16
VOLUME = NX * NY * NZ * NT
F32, BF16 = jnp.float32, jnp.bfloat16
MIB = 1024 * 1024


def signed(index, modes):
    return np.where(index < modes // 2, index, index - modes)


def hi_lo(table):
    hi = table.astype(np.float32).astype(ml_dtypes.bfloat16)
    lo = (table - hi.astype(np.float64)).astype(np.float32).astype(ml_dtypes.bfloat16)
    return hi, lo


def y_table():
    angle = 2 * np.pi * np.arange(NY) / NY
    rows = np.zeros((2, 16, NY))
    for parity in range(2):
        for k in range(7):
            rows[parity, 4 * parity + k] = np.cos(k * angle)
        for k in range(1, 6):
            rows[parity, 4 * parity + 6 + k] = -np.sin(k * angle)
        rows[parity, LAST_SINE[parity]] = np.sin(6 * angle)
    return np.einsum("prv,xz->pxrvz", rows, np.eye(SLAB)).reshape(2, 16 * SLAB, NY * SLAB)


def plane_table():
    z = np.arange(PLANE) // NT
    t = np.arange(PLANE) % NT
    rows = []
    for ql in range(2):
        q = 2 * np.arange(OWNERS) + ql
        fz = signed(q // MT, MZ)[:, None]
        ft = signed(q % MT, MT)[:, None]
        phase = (fz * z * NT + ft * t * NZ) % PLANE
        theta = 2 * np.pi * phase / PLANE
        rows.append(np.concatenate([np.cos(theta), np.sin(theta)], axis=1))
        rows.append(np.concatenate([-np.sin(theta), np.cos(theta)], axis=1))
    return np.concatenate(rows, axis=0)


def x_table(ql):
    lane = np.arange(256) + 128 * ql
    f = signed(lane % MX, MX)[None, :]
    theta = 2 * np.pi * ((f * np.arange(NX)[:, None]) % NX) / NX
    cos, sin = np.cos(theta), np.sin(theta)
    rows = [np.concatenate([cos, -sin], axis=1), np.concatenate([sin, cos], axis=1)]
    return np.stack(rows, axis=1).reshape(2 * NX, 512)


def mode_mask():
    fold = np.zeros((MY, MY), np.float32)
    fold[0, 0] = fold[6, 6] = 1.0
    for k in range(1, 6):
        fold[k, k] = fold[k, MY - k] = fold[6 + k, k] = 1.0
        fold[6 + k, MY - k] = -1.0
    mask = np.zeros((2, 24, 512), np.float32)
    for ql in range(2):
        lane = np.arange(256) + 128 * ql
        code = np.where(lane < 288, lane // MX, -1)
        here = code // MY == ql
        half = np.where(here[None, :], fold[np.arange(24) % MY][:, code % MY], 0.0)
        mask[ql] = np.concatenate([half, half], axis=1)
    return mask


def group_table():
    g = np.zeros((CP, KEPT_ROWS), np.float32)
    for c in range(C):
        g[c, c * MY : (c + 1) * MY] = 1.0
    return g


def split(value):
    hi = value.astype(BF16)
    return hi, (value - hi.astype(F32)).astype(BF16)


def dot(a, b):
    return lax.dot_general(a, b, (((1,), (0,)), ((), ())), preferred_element_type=F32)


def dot_tn(a, b):
    return lax.dot_general(a, b, (((0,), (0,)), ((), ())), preferred_element_type=F32)


def dot_nt(a, b):
    return lax.dot_general(a, b, (((1,), (1,)), ((), ())), preferred_element_type=F32)


def folded_rows(parity):
    return lax.broadcasted_iota(jnp.int32, (16, 128), 0) - 4 * parity


def forward_y(quad, cells, ytab, u_ref):
    for parity in range(2):
        first = 4 * quad + parity
        left, right = cells(first), cells(first + 2)
        table = ytab[parity]
        u = dot(table, jnp.concatenate([left[0], right[0]], axis=1))
        u = u[:64] + u[64:]
        if len(left) > 1:
            u = u + dot(table[:64], jnp.concatenate([left[1], right[1]], axis=1))
        k = folded_rows(parity)
        kept = slice(4 * parity, 4 * parity + MY)
        for side in range(2):
            at = (first + 2 * side) * MY
            for x in range(SLAB):
                group = u[x * 16 : (x + 1) * 16, side * 128 : (side + 1) * 128]
                sine = group[LAST_SINE[parity] : LAST_SINE[parity] + 1]
                real = jnp.where(k <= 6, group, 0.0)
                imag = jnp.where(k >= 7, group, jnp.where(k == 6, sine, 0.0))
                u_ref[x, at : at + MY, :128] = real[kept]
                u_ref[x, at : at + MY, 128:] = imag[kept]


def forward_plane(u_ref, ztab, out_ref):
    for x in range(SLAB):
        u_ref[x, KEPT_ROWS:, :] = jnp.zeros((256 - KEPT_ROWS, 256), F32)
        hi, lo = split(u_ref[x])
        both = dot_nt(ztab[...], hi)
        out = both[:64] + both[64:] + dot_nt(ztab[:64], lo)
        for ql in range(2):
            for reim in range(2):
                at = (ql * 2 + reim) * 16
                for half in range(2):
                    start = (ql * 2 + half) * 8 + x * 2 + reim
                    out_ref[pl.ds(start, OWNERS, stride=32), :] = out[at : at + 16, half * 128 : (half + 1) * 128]


def inverse_plane(recv_ref, ztab_k, h_ref):
    for x in range(SLAB):
        parts = []
        for ql in range(2):
            for reim in range(2):
                halves = [
                    recv_ref[pl.ds((ql * 2 + half) * 8 + x * 2 + reim, OWNERS, stride=32), :] for half in range(2)
                ]
                parts.append(jnp.concatenate(halves, axis=1))
        hi, lo = split(jnp.concatenate(parts, axis=0))
        h_ref[x] = dot_tn(jnp.concatenate([hi, lo, hi], axis=0), ztab_k[...])


def inverse_y(quad, h_ref, ytab_t):
    out = [None] * 4
    for parity in range(2):
        k = folded_rows(parity)
        last = LAST_SINE[parity] - 4 * parity
        sides = []
        for side in range(2):
            at = (4 * quad + parity + 2 * side) * MY - 4 * parity
            groups = []
            for x in range(SLAB):
                imag = h_ref[x, at : at + 16, 128:]
                sine = imag[4 * parity + 6 : 4 * parity + 7]
                group = jnp.where(k <= 6, h_ref[x, at : at + 16, :128], imag)
                groups.append(jnp.where(k == last, sine, group))
            sides.append(jnp.concatenate(groups, axis=0))
        hi, lo = split(jnp.concatenate(sides, axis=1))
        both = dot(ytab_t[parity], jnp.concatenate([hi, lo, hi], axis=0))
        out[parity], out[parity + 2] = both[:, :128], both[:, 128:]
    return out


def quad_rows(quad):
    return pl.ds(quad * QUAD_ROWS, QUAD_ROWS)


def fetch(source, target, sems, first):
    copies = [
        pltpu.make_async_copy(source.at[quad_rows(q)], target.at[quad_rows(q)], sems.at[first + q])
        for q in range(STEPS)
    ]
    return copies


def forward_kernel(x_hbm, ytab_hbm, ztab_hbm, out_ref, x_ref, ytab, ztab, u_ref, sems):
    tables = [
        pltpu.make_async_copy(ytab_hbm, ytab, sems.at[STEPS]),
        pltpu.make_async_copy(ztab_hbm, ztab, sems.at[STEPS + 1]),
    ]
    copies = fetch(x_hbm, x_ref, sems, 0)
    for copy in [copies[0], tables[0]] + copies[1:] + [tables[1]]:
        copy.start()
    tables[0].wait()
    for quad in range(STEPS):
        copies[quad].wait()
        forward_y(quad, lambda c: [x_ref[c * CELL_ROWS : (c + 1) * CELL_ROWS, :]], ytab, u_ref)
    tables[1].wait()
    forward_plane(u_ref, ztab, out_ref)


def invert(quad, h_ref, ytab_t, pre_ref):
    for k, block in enumerate(inverse_y(quad, h_ref, ytab_t)):
        at = (4 * quad + k) * CELL_ROWS
        pre_ref[at : at + CELL_ROWS, :] = block


def middle_kernel(
    recv_ref, local_hbm, cot_hbm, ytab, ztab, ytab_t, ztab_k,
    act_hbm, up_hbm, out_ref,
    local_ref, cot_ref, act_ref, up_ref, h_ref, u_ref, pre_ref, hi_ref, lo_ref, sems,
):
    local_copies = fetch(local_hbm, local_ref, sems, 0)
    cot_copies = fetch(cot_hbm, cot_ref, sems, STEPS)
    for pair in zip(local_copies, cot_copies):
        for copy in pair:
            copy.start()
    stores = []
    inverse_plane(recv_ref, ztab_k, h_ref)
    for quad in range(AHEAD):
        invert(quad, h_ref, ytab_t, pre_ref)
    for quad in range(STEPS):
        if quad + AHEAD < STEPS:
            invert(quad + AHEAD, h_ref, ytab_t, pre_ref)
        local_copies[quad].wait()
        cot_copies[quad].wait()
        for i in range(QUAD_ROWS // CHUNK):
            near = slice(i * CHUNK, (i + 1) * CHUNK)
            rows = slice(quad * QUAD_ROWS + i * CHUNK, quad * QUAD_ROWS + (i + 1) * CHUNK)
            pre = pre_ref[rows, :] + local_ref[rows, :]
            cdf = 0.5 * (1.0 + lax.erf(pre * (1.0 / math.sqrt(2.0))))
            slope = cdf + pre * jnp.exp(-0.5 * pre * pre) * (1.0 / math.sqrt(2.0 * math.pi))
            act_ref[rows, :] = (pre * cdf).astype(BF16)
            up = cot_ref[rows, :].astype(F32) * slope
            up_ref[rows, :] = up
            hi_ref[near, :], lo_ref[near, :] = split(up)
        for k, (source, target) in enumerate(((act_ref, act_hbm), (up_ref, up_hbm))):
            store = pltpu.make_async_copy(
                source.at[quad_rows(quad)], target.at[quad_rows(quad)], sems.at[(2 + k) * STEPS + quad]
            )
            store.start()
            stores.append(store)
        def parts(c):
            rows = slice((c - 4 * quad) * CELL_ROWS, (c - 4 * quad + 1) * CELL_ROWS)
            return [hi_ref[rows, :], lo_ref[rows, :]]

        forward_y(quad, parts, ytab, u_ref)
    forward_plane(u_ref, ztab, out_ref)
    for store in stores:
        store.wait()


def weight_kernel(own_ref, far_ref, near1_ref, near2_ref, near3_ref, _, grad_ref, a_ref):
    near_refs = [near1_ref, near2_ref, near3_ref]
    even = lax.broadcasted_iota(jnp.int32, (2 * C, 128), 0) % 2 == 0
    terms = []
    for s, ref in enumerate([own_ref, far_ref.at[0]] + [ref.at[k] for ref in near_refs for k in range(2)]):
        block = ref[...]
        a_ref[s] = block
        b = pltpu.roll(block, 64, 1)
        below, above = pltpu.roll(b, 2 * C - 1, 0), pltpu.roll(b, 1, 0)
        terms.append((b, jnp.where(even, below, -above)))
    for c in range(C):
        total = jnp.zeros((2 * C, 128), F32)
        for s, (b, swapped) in enumerate(terms):
            total = total + (a_ref[s, 2 * c : 2 * c + 1, :] * b + a_ref[s, 2 * c + 1 : 2 * c + 2, :] * swapped)
        grad_ref[c * 2 * C : (c + 1) * 2 * C, :] = total[:, :BLOCK_MODES]


def last_kernel(recv_ref, local_hbm, ytab_t, ztab_k, out_hbm, token_ref, local_ref, out_ref, pre_ref, h_ref, sems):
    token_ref[...] = jnp.zeros_like(token_ref)
    local_copies = fetch(local_hbm, local_ref, sems, 0)
    for copy in local_copies:
        copy.start()
    stores = []
    inverse_plane(recv_ref, ztab_k, h_ref)
    for quad in range(AHEAD):
        invert(quad, h_ref, ytab_t, pre_ref)
    for quad in range(STEPS):
        if quad + AHEAD < STEPS:
            invert(quad + AHEAD, h_ref, ytab_t, pre_ref)
        local_copies[quad].wait()
        for k in range(4):
            at = (4 * quad + k) * CELL_ROWS
            rows = slice(at, at + CELL_ROWS)
            out_ref[rows, :] = (pre_ref[rows, :] + local_ref[rows, :]).astype(BF16)
        store = pltpu.make_async_copy(
            out_ref.at[quad_rows(quad)], out_hbm.at[quad_rows(quad)], sems.at[STEPS + quad]
        )
        store.start()
        stores.append(store)
    for store in stores:
        store.wait()


def point_kernel(transposed, x_ref, w_ref, *rest):
    bias_ref, out_ref, token_ref = rest if len(rest) == 3 else (None, *rest)
    token_ref[...] = jnp.zeros_like(token_ref)
    size = C * MIX
    row = lax.broadcasted_iota(jnp.int32, (size, C), 0)
    spread = (row // MIX == lax.broadcasted_iota(jnp.int32, (size, C), 1)).astype(F32)
    offset = jnp.sum(spread * bias_ref[...], axis=1, keepdims=True) if bias_ref is not None else 0.0
    spread = spread.astype(BF16)
    wide = (dot_nt if transposed else dot)(spread, w_ref[...]).astype(BF16)
    wide = dot_nt(wide, spread)
    row = lax.broadcasted_iota(jnp.int32, (size, size), 0)
    column = lax.broadcasted_iota(jnp.int32, (size, size), 1)
    wide = jnp.where(row % MIX == column % MIX, wide, 0.0).astype(BF16)
    for block in range(SLAB * NY // (2 * MIX)):
        sides = []
        for side in range(2):
            at = (2 * block + side) * MIX
            sides.append(
                jnp.concatenate([x_ref[c * SLAB * NY + at : c * SLAB * NY + at + MIX, :] for c in range(C)], axis=0)
            )
        both = jnp.concatenate(sides, axis=1)
        if both.dtype == BF16:
            out = dot(wide, both)
        else:
            hi, lo = split(both)
            out = dot(wide, hi) + dot(wide, lo)
        out = out + offset
        for side in range(2):
            at = (2 * block + side) * MIX
            for c in range(C):
                out_ref[c * SLAB * NY + at : c * SLAB * NY + at + MIX, :] = out[
                    c * MIX : (c + 1) * MIX, side * 128 : (side + 1) * 128
                ]


def owner_kernel(adjoint, s_ref, w_hbm, xhi, xlo, mask_ref, g_ref, *rest):
    *rest, w_ref, w_sem, out_ref, out_sems = rest
    fetch_w = pltpu.make_async_copy(w_hbm, w_ref, w_sem)
    fetch_w.start()
    if adjoint:
        first_ref, _, out_hbm, *send_refs = rest[:8]
        f_ref, m_ref, turn_ref, b_ref = rest[8:]
        send_refs = send_refs[:4] + [send_refs[4].at[k] for k in range(4)]
    else:
        out_hbm, spec_hbm, f_ref, m_ref, turn_ref, spec_ref, sem = rest
        store = pltpu.make_async_copy(spec_ref, spec_hbm, sem)
    g = g_ref[...]
    halves = []
    for ql in range(2):
        tiles = [s_ref[:, t * 8 : (t + 1) * 8, :].reshape(128, 128) for t in (2 * ql, 2 * ql + 1)]
        hi, lo = split(jnp.concatenate(tiles, axis=1))
        top = xhi[ql]
        rep = dot_tn(jnp.concatenate([hi, lo], axis=0), jnp.concatenate([top, top], axis=0)) + dot_tn(hi, xlo[ql])
        rep = rep[:KEPT_ROWS].reshape(PAIRS, 24, 512) * mask_ref[ql][None]
        hi, lo = split(rep.reshape(KEPT_ROWS, 512))
        halves.append(dot(g, hi) + dot(g, lo))
    for reim in range(2):
        a = halves[0][:, reim * 256 : (reim + 1) * 256]
        b = halves[1][:, reim * 256 : (reim + 1) * 256]
        joined = jnp.concatenate([a[:, :128], a[:, 128:] + b[:, :128], b[:, 128:]], axis=1)
        f_ref[reim] = joined * (1.0 / VOLUME) if adjoint else joined
    for reim in range(2):
        for t in range(3):
            turn_ref[t, pl.ds(reim, CP, stride=2), :] = f_ref[reim, :, t * 128 : (t + 1) * 128]
    turned = jnp.concatenate([turn_ref[t, : 2 * C, :] for t in range(3)], axis=1)
    for j in range(SAMPLES):
        block = turned[:, j * BLOCK_MODES : (j + 1) * BLOCK_MODES]
        if adjoint:
            b_ref[j, :, 64 : 64 + BLOCK_MODES] = block
            b_ref[j, :, :BLOCK_MODES] = first_ref[j, :, :BLOCK_MODES]
        else:
            spec_ref[j, :, :BLOCK_MODES] = block
    if adjoint:
        me = lax.axis_index("sample")
        for d in range(SAMPLES):
            send_refs[d][...] = b_ref[jnp.bitwise_xor(me, NEAR[d % 4] + FAR * (d // 4))]
    else:
        store.start()
    m_ref[...] = jnp.zeros_like(m_ref)
    fetch_w.wait()
    if adjoint:
        fr, fi = f_ref[0, :C, :288], f_ref[1, :C, :288]
        for c in range(C):
            wr, wi = w_ref[c].astype(F32), w_ref[C + c].astype(F32)
            m_ref[0, c : c + 1, :288] = jnp.sum(wr * fr + wi * fi, axis=0, keepdims=True)
            m_ref[1, c : c + 1, :288] = jnp.sum(wr * fi - wi * fr, axis=0, keepdims=True)
    else:
        mr = jnp.zeros((C, 288), F32)
        mi = jnp.zeros((C, 288), F32)
        for c in range(C):
            wr, wi = w_ref[c].astype(F32), w_ref[C + c].astype(F32)
            fr, fi = f_ref[0, c : c + 1, :288], f_ref[1, c : c + 1, :288]
            mr = mr + (wr * fr - wi * fi)
            mi = mi + (wr * fi + wi * fr)
        m_ref[0, :C, :288] = mr * (1.0 / VOLUME)
        m_ref[1, :C, :288] = mi * (1.0 / VOLUME)
    sent = []
    upper = lax.broadcasted_iota(jnp.int32, (24, 256), 0) < MY
    for ql in range(2):
        lanes = slice(ql * 128, ql * 128 + 256)
        mask = mask_ref[ql]
        rows = []
        for c in range(0, C, 2):
            pair = []
            for reim in range(2):
                even, odd = m_ref[reim, c : c + 1, lanes], m_ref[reim, c + 1 : c + 2, lanes]
                pair.append(jnp.where(upper, even, odd))
            rows.append(jnp.concatenate(pair, axis=1) * mask)
        rows.append(jnp.zeros((256 - KEPT_ROWS, 512), F32))
        hi, lo = split(jnp.concatenate(rows, axis=0))
        both = dot_nt(jnp.concatenate([xhi[ql], xlo[ql]], axis=0), hi)
        out = both[:128] + both[128:] + dot_nt(xhi[ql], lo)
        for half in range(2):
            t = 2 * ql + half
            out_ref[:, t * 8 : (t + 1) * 8, :] = out[:, half * 128 : (half + 1) * 128].reshape(OWNERS, 8, 128)
        part = (slice(None), pl.ds(ql * 16, 16), slice(None))
        sent.append(pltpu.make_async_copy(out_ref.at[part], out_hbm.at[part], out_sems.at[ql]))
        sent[ql].start()
    for copy in sent:
        copy.wait()
    if not adjoint:
        store.wait()


def whole(shape):
    return pl.BlockSpec(shape, lambda *_: (0,) * len(shape))


def pinned():
    return pl.BlockSpec(memory_space=pltpu.HBM)


def params(limit):
    return pltpu.CompilerParams(vmem_limit_bytes=int(limit * MIB))


def cost(us):
    return pl.CostEstimate(flops=int(us * 4e8), bytes_accessed=int(us * 3e6), transcendentals=0)


def exchange(block):
    return lax.all_to_all(block, "space", split_axis=0, concat_axis=0, tiled=True)


def shards(fields, cotangent, spectral_weight, point_weight, point_bias):
    yhi, ylo = hi_lo(y_table())
    zhi, zlo = hi_lo(plane_table())
    ytab = jnp.asarray(np.concatenate([yhi, ylo], axis=1))
    ztab = jnp.asarray(np.concatenate([zhi, zlo], axis=0))
    yhi_t, ylo_t = (np.swapaxes(t, 1, 2) for t in (yhi, ylo))
    ytab_t = jnp.asarray(np.concatenate([yhi_t, yhi_t, ylo_t], axis=2))
    ztab_k = jnp.asarray(np.concatenate([zhi, zhi, zlo], axis=0))
    mask = jnp.asarray(mode_mask())
    g = jnp.asarray(group_table().astype(ml_dtypes.bfloat16))
    xhi, xlo = map(jnp.asarray, hi_lo(np.stack([x_table(ql) for ql in range(2)])))
    flat = (OWNERS * 32, 128)
    slab_out = jax.ShapeDtypeStruct(flat, F32)
    owned_out = jax.ShapeDtypeStruct((OWNERS, 32, 128), F32)
    rows_out = [jax.ShapeDtypeStruct((ROWS, 128), dtype) for dtype in (BF16, F32)]
    table_specs = [whole(ytab.shape), whole(ztab.shape)]
    inverse_specs = [whole(ytab_t.shape), whole(ztab_k.shape)]
    planes = pltpu.VMEM((SLAB, 256, 256), F32)

    def owner(received, adjoint, *first):
        weights = spectral_weight.reshape(2 * C, C, 288)
        if adjoint:
            spec_shapes = [(2 * C, 128)] * 4 + [(4, 2 * C, 128)]
        else:
            spec_shapes = [(SAMPLES, 2 * C, 128)]
        scratch = [pltpu.VMEM((2, CP, 384), F32), pltpu.VMEM((2, CP, 384), F32), pltpu.VMEM((3, 2 * CP, 128), F32)]
        scratch.append(pltpu.VMEM((SAMPLES, 2 * C, 128), F32))
        operands = [received, weights, xhi, xlo, mask, g, *first]
        in_specs = [pinned() if k == 1 else whole(o.shape) for k, o in enumerate(operands)]
        if not adjoint:
            scratch.append(pltpu.SemaphoreType.DMA)
        return pl.pallas_call(
            functools.partial(owner_kernel, adjoint),
            out_shape=[owned_out] + [jax.ShapeDtypeStruct(shape, F32) for shape in spec_shapes],
            in_specs=in_specs,
            scratch_shapes=scratch
            + [pltpu.VMEM((2 * C, C, 288), BF16), pltpu.SemaphoreType.DMA]
            + [pltpu.VMEM(owned_out.shape, F32), pltpu.SemaphoreType.DMA((2,))],
            out_specs=[pinned()] + (list(map(whole, spec_shapes)) if adjoint else [pinned()]),
            compiler_params=params(52),
            cost_estimate=cost(3),
            name="owner_up" if adjoint else "owner_in",
        )(*operands)

    def as_rows(array):
        return jnp.transpose(array.reshape(SLAB, C, NY, PLANE), (1, 2, 0, 3)).reshape(ROWS, PLANE)

    def as_planes(rows):
        return jnp.transpose(rows.reshape(C, NY, SLAB, PLANE), (2, 0, 1, 3)).reshape(1, SLAB, C, CELLS)

    def point(values, transposed, *bias):
        return pl.pallas_call(
            functools.partial(point_kernel, transposed),
            out_shape=[rows_out[1], jax.ShapeDtypeStruct((8, 128), F32)],
            compiler_params=params(24),
            cost_estimate=cost(4),
            name="point_in" if transposed else "point_up",
        )(values, point_weight, *bias)

    field_rows = as_rows(fields)
    sems = pltpu.SemaphoreType.DMA
    sent = pl.pallas_call(
        forward_kernel,
        in_specs=[pinned()] * 3,
        out_shape=slab_out,
        scratch_shapes=[
            pltpu.VMEM((ROWS, 128), BF16), pltpu.VMEM(ytab.shape, BF16), pltpu.VMEM(ztab.shape, BF16),
            planes, sems((STEPS + 2,)),
        ],
        compiler_params=params(56),
        cost_estimate=cost(3),
        name="slab_in",
    )(field_rows, ytab, ztab)
    mixed, spec_in = owner(exchange(sent.reshape(OWNERS, 32, 128)), False)
    local, _ = point(field_rows, True, point_bias[None, :])
    activated, upstream, sent = pl.pallas_call(
        middle_kernel,
        in_specs=[whole(flat), pinned(), pinned()] + table_specs + inverse_specs,
        out_specs=[pinned(), pinned(), whole(flat)],
        out_shape=rows_out + [slab_out],
        scratch_shapes=[pltpu.VMEM((ROWS, 128), dtype) for dtype in (F32, BF16, BF16, F32)]
        + [planes, planes, pltpu.VMEM((ROWS, 128), F32)]
        + [pltpu.VMEM((QUAD_ROWS, 128), BF16)] * 2
        + [sems((4 * STEPS,))],
        compiler_params=params(52),
        cost_estimate=cost(8),
        name="slab_mid",
    )(exchange(mixed).reshape(flat), local, as_rows(cotangent), ytab, ztab, ytab_t, ztab_k)
    local, token = point(upstream, False)
    back, *sends = owner(exchange(sent.reshape(OWNERS, 32, 128)), True, spec_in, token)
    def swap(block, bits):
        return lax.ppermute(block, "sample", [(s, s ^ bits) for s in range(SAMPLES)])

    far = swap(sends[4], FAR)
    near = [swap(jnp.stack([sends[k], far[k]]), NEAR[k]) for k in range(1, 4)]
    grad_input, done = pl.pallas_call(
        last_kernel,
        in_specs=[whole(flat), pinned()] + inverse_specs,
        out_specs=[pinned(), whole((8, 128))],
        out_shape=[rows_out[0], jax.ShapeDtypeStruct((8, 128), F32)],
        scratch_shapes=[pltpu.VMEM((ROWS, 128), dtype) for dtype in (F32, BF16, F32)] + [planes, sems((2 * STEPS,))],
        compiler_params=params(52),
        cost_estimate=cost(20),
        name="slab_out",
    )(exchange(back).reshape(flat), local, ytab_t, ztab_k)
    grad_spectral = pl.pallas_call(
        weight_kernel,
        out_shape=jax.ShapeDtypeStruct((2 * C * C, BLOCK_MODES), F32),
        scratch_shapes=[pltpu.VMEM((SAMPLES, 2 * C, 128), F32)],
        compiler_params=params(8),
        cost_estimate=cost(1),
        name="weight_grad",
    )(sends[0], far, *near, done)
    grad_spectral = jnp.transpose(grad_spectral.reshape(C, C, 2, BLOCK_MODES), (2, 0, 1, 3))
    return as_planes(activated), as_planes(grad_input), grad_spectral


def solution(mesh):
    return jax.shard_map(
        shards,
        mesh=mesh,
        in_specs=(
            P("sample", "space", None, None),
            P("sample", "space", None, None),
            P(None, None, None, "space"),
            P(),
            P(),
        ),
        out_specs=(
            P("sample", "space", None, None),
            P("sample", "space", None, None),
            P(None, None, None, ("space", "sample")),
        ),
        check_vma=False,
    )
```
